512 devices in a mesh: tiles: 32 (over z, core), dp: 16 (over y, x).
Axes of the slice: x: 4, y: 4, z: 16, core: 2. Of those that a mesh axis runs over, the one named last changes fastest.
Arguments:
- fields: bfloat16 [16, 64, 32, 32, 256], P('dp', 'tiles'), may hold values from -6 to 6
- neighbours: int32 [64, 8], P('tiles'), may hold values from -1 to 63, as said below
- kernel: float32 [7, 7, 256], replicated, may hold values from -0.875 to 0.875
- gain: float32 [256], replicated, may hold values from 0.1 to 1.9
- w_in: bfloat16 [256, 1024], replicated, may hold values from -0.375 to 0.375
- w_out: bfloat16 [1024, 256], replicated, may hold values from -0.1875 to 0.1875
- cotangent: bfloat16 [16, 64, 32, 32, 256], P('dp', 'tiles'), may hold values from -6 to 6
Outputs:
- grad_fields: bfloat16 [16, 64, 32, 32, 256], P('dp', 'tiles')
- grad_w_in: float32 [256, 1024], P(None, 'dp')
- grad_w_out: float32 [1024, 256], P('dp')
- grad_kernel: float32 [7, 7, 256], replicated
- gradient_by_gain: float32 [256], replicated
The draws below stay inside these ranges and needn't reach their ends.
Inputs may be any that keep to these rules, and one draw needn't show every extreme that they name: `neighbours`: wet tiles of a slab of 3 rows and 32 columns (longitude wraps), numbered column by column; a neighbour's slot differs from the tile's own by at most 4 around the slot order, and this distance is reached; the relation is symmetric (b is a's neighbour in a direction exactly when a is b's in the opposite one).
All inputs are finite; a program needn't handle non-finite values.
Results may differ from the reference program's by a relative error of at most 0.0056.
Values may be sent and summed in bfloat16 or wider, within the bound.
No kernel may reach another device: no remote copies, remote signals or barrier semaphores. Data moves between devices by JAX's collectives and lax.ppermute only.
A program may use at most 64 MiB of HBM per device.

```python
import jax
import jax.numpy as jnp
from jax import lax

C = 256
FF = 1024
TILE = 32
KW = 7
GY = 3
SAMPLES = 16
SLOTS = 64
COLUMNS = 32


def draw_neighbours(key, part):
    key = jax.random.fold_in(key, 11)
    key_count, key_rows = jax.random.split(key)
    pairs = COLUMNS // 2
    first = jax.random.randint(key_count, (pairs,), 0, 3)
    first = first.at[0].set(2)
    first = first.at[1].set(0)
    land_count = jnp.stack([first, 2 - first], axis=1).reshape(COLUMNS)
    scores = jax.random.randint(key_rows, (COLUMNS, GY), 0, 1 << 20) * GY + jnp.arange(GY)[None, :]
    order = jnp.argsort(scores, axis=1)
    place = jnp.argsort(order, axis=1)
    wet = (place >= land_count[:, None]).astype(jnp.int32)
    flat_wet = wet.reshape(-1)
    ranks = jnp.cumsum(flat_wet) - 1
    rank_grid = jnp.where(wet > 0, ranks.reshape(COLUMNS, GY), -1)
    row_ids = jnp.arange(GY)
    col_ids = jnp.arange(COLUMNS)
    moves = [(-1, 0), (1, 0), (0, -1), (0, 1), (-1, -1), (-1, 1), (1, -1), (1, 1)]
    lists = []
    for drow, dcol in moves:
        near_row = row_ids[None, :] + drow
        near_col = (col_ids[:, None] + dcol) % COLUMNS
        inside = (near_row >= 0) & (near_row < GY)
        value = rank_grid[near_col, jnp.clip(near_row, 0, GY - 1)]
        lists.append(jnp.where(inside, value, -1))
    table = jnp.stack(lists, axis=-1).reshape(COLUMNS * GY, 8)
    target = jnp.where(flat_wet > 0, ranks, SLOTS)
    result = jnp.full((SLOTS, 8), -1, jnp.int32).at[target].set(table.astype(jnp.int32), mode='drop')
    return result.astype(jnp.int32)


def block_scale(stream_key, dims, pieces, low, high):
    factor_of = 1.0
    for dim, blocks in pieces:
        heights = jax.random.uniform(jax.random.fold_in(jax.random.fold_in(stream_key, 6), dim), (blocks,), jnp.float32, low / len(pieces), high / len(pieces))
        factor_of = factor_of * jnp.repeat(jnp.exp(heights), dims[dim] // blocks).reshape((-1,) + (1,) * (len(dims) - 1 - dim))
    return factor_of


def gaussian(key, shape, scale, most, shards=(), kind=jnp.bfloat16):
    values = jax.random.normal(key, shape, jnp.float32) * scale
    if len(shards) > 0:
        values = block_scale(key, shape, shards, -0.22, 0.18) * values
    return jnp.clip(values, min=-most, max=most).astype(kind)


def setup_inputs(seed: int = 0) -> dict:
    keys = jax.random.split(jax.random.key(seed), 8)
    fields = gaussian(keys[0], (SAMPLES, SLOTS, TILE, TILE, C), 1.0, 6.0, ((0, 16), (1, 32)))
    neighbours = draw_neighbours(jax.random.fold_in(keys[7], 71), 0)
    kernel = gaussian(keys[2], (KW, KW, C), (KW * KW) ** -0.5, 0.875, (), jnp.float32)
    gain = jnp.clip(1.0 + 0.18 * jax.random.normal(keys[3], (C,), jnp.float32), 0.1, 1.9)
    w_in = gaussian(keys[4], (C, FF), C ** -0.5, 0.375)
    w_out = gaussian(keys[5], (FF, C), FF ** -0.5, 0.1875)
    cotangent = gaussian(keys[6], (SAMPLES, SLOTS, TILE, TILE, C), 1.0, 6.0, ((0, 16), (1, 32)))
    return {"fields": fields, "neighbours": neighbours, "kernel": kernel, "gain": gain, "w_in": w_in, "w_out": w_out, "cotangent": cotangent}


def rims_of(tiles):
    top = tiles[..., :3, :, :]
    bottom = tiles[..., -3:, :, :]
    left = jnp.swapaxes(tiles[..., :, :3, :], -3, -2)
    right = jnp.swapaxes(tiles[..., :, -3:, :], -3, -2)
    return jnp.stack([top, bottom, left, right], axis=-4)

def assemble(tiles, near):
    north = near[..., 0, 1, :, :, :]
    south = near[..., 1, 0, :, :, :]
    west = jnp.swapaxes(near[..., 2, 3, :, :, :], -3, -2)
    east = jnp.swapaxes(near[..., 3, 2, :, :, :], -3, -2)
    corner_nw = near[..., 4, 1, :, -3:, :]
    corner_ne = near[..., 5, 1, :, :3, :]
    corner_sw = near[..., 6, 0, :, -3:, :]
    corner_se = near[..., 7, 0, :, :3, :]
    upper = jnp.concatenate([corner_nw, north, corner_ne], axis=-2)
    middle = jnp.concatenate([west, tiles, east], axis=-2)
    lower = jnp.concatenate([corner_sw, south, corner_se], axis=-2)
    return jnp.concatenate([upper, middle, lower], axis=-3)

def depthwise(padded, kern, size):
    total = jnp.zeros(padded.shape[:-3] + (size, size, padded.shape[-1]), jnp.float32)
    for row in range(KW):
        for col in range(KW):
            total = total + padded[..., row:row + size, col:col + size, :] * kern[row, col]
    return total

def gelu_exact(value):
    return jax.nn.gelu(value, approximate=False)

def reference(fields, neighbours, kernel, gain, w_in, w_out, cotangent):
    valid = neighbours >= 0
    picked = jnp.where(valid, neighbours, 0).astype(jnp.int32)
    size = fields.shape[2]

    def widen(tiles):
        near = rims_of(tiles)[picked]
        near = jnp.where(valid[:, :, None, None, None, None], near, jnp.zeros((), tiles.dtype))
        return assemble(tiles, near)

    def one_sample(pair):
        tiles, grad_out = pair
        padded = widen(tiles)
        convolved_state = depthwise(padded, kernel, size)
        channel_mean = lax.optimization_barrier(jnp.mean(convolved_state, axis=-1, keepdims=True))
        var = lax.optimization_barrier(jnp.mean((convolved_state - channel_mean) ** 2, axis=-1, keepdims=True))
        inverse_deviation = lax.rsqrt(var + 1e-06)
        centered_standardized = (convolved_state - channel_mean) * inverse_deviation
        layer_normalized = (centered_standardized * gain).astype(jnp.bfloat16)
        rows_n = layer_normalized.reshape(-1, layer_normalized.shape[-1])
        pre = jnp.dot(rows_n, w_in, preferred_element_type=jnp.float32)
        act = gelu_exact(pre).astype(jnp.bfloat16)
        rows_g = grad_out.reshape(-1, grad_out.shape[-1])
        gw_out = lax.dot_general(act, rows_g, (((0,), (0,)), ((), ())), preferred_element_type=jnp.float32)
        grad_act = lax.dot_general(rows_g, w_out, (((1,), (1,)), ((), ())), preferred_element_type=jnp.float32)
        pullback = jax.vjp(gelu_exact, pre)[1]
        grad_pre = pullback(grad_act)[0].astype(jnp.bfloat16)
        gw_in_t = lax.dot_general(grad_pre, rows_n, (((0,), (0,)), ((), ())), preferred_element_type=jnp.float32)
        normalized_gradient = lax.dot_general(grad_pre, w_in, (((1,), (1,)), ((), ())), preferred_element_type=jnp.float32)
        normalized_gradient = normalized_gradient.reshape(convolved_state.shape)
        gradient_by_gain = lax.optimization_barrier(jnp.sum(normalized_gradient * centered_standardized, axis=(0, 1, 2)))
        gain_scaled = normalized_gradient * gain
        convolved_gradient = inverse_deviation * (gain_scaled - lax.optimization_barrier(jnp.mean(gain_scaled, axis=-1, keepdims=True)) - centered_standardized * lax.optimization_barrier(jnp.mean(gain_scaled * centered_standardized, axis=-1, keepdims=True)))
        convolved_gradient = convolved_gradient.astype(jnp.bfloat16)
        conv_f = convolved_gradient.astype(jnp.float32)
        kern_rows = []
        for row in range(KW):
            for col in range(KW):
                piece = padded[:, row:row + size, col:col + size, :].astype(jnp.float32)
                kern_rows.append(lax.optimization_barrier(jnp.sum(piece * conv_f, axis=(0, 1, 2))))
        grad_kernel = jnp.stack(kern_rows, axis=0).reshape(KW, KW, -1)
        grad_padded = widen(convolved_gradient)
        grad_x = depthwise(grad_padded, kernel[::-1, ::-1], size)
        grad_tiles = (grad_out.astype(jnp.float32) + grad_x).astype(jnp.bfloat16)
        return (grad_tiles, gw_in_t, gw_out, grad_kernel, gradient_by_gain)
    grads, gw_in_t, gw_out, gkern, ggain = lax.map(one_sample, (fields, cotangent))
    scale = 1.0 / jnp.sqrt(jnp.float32(fields.shape[0] * fields.shape[1] * size * size))
    grad_w_in = lax.optimization_barrier(jnp.sum(gw_in_t, axis=0)).T * scale
    grad_w_out = lax.optimization_barrier(jnp.sum(gw_out, axis=0)) * scale
    return (grads, grad_w_in, grad_w_out, lax.optimization_barrier(jnp.sum(gkern, axis=0)) * scale, lax.optimization_barrier(jnp.sum(ggain, axis=0)) * scale)
```

```python
import functools

import jax
import jax.numpy as jnp
from jax import lax
from jax.experimental import pallas as pl
from jax.experimental.pallas import tpu as pltpu
from jax.sharding import PartitionSpec as P

KW = 7
TAPS = KW * KW
RIM = KW // 2
SIZE = 32
WIDE = SIZE + 2 * RIM
HALF = SIZE // 2
TALL = HALF + 2 * RIM
CH = 256
FF = 1024
ROWS = 256
VMEM_LIMIT = 56 * 1024 * 1024
F32 = jnp.float32
BF16 = jnp.bfloat16
OFFSETS = (0, -1, 1, -2, 2)
PAIRS = (
    ((0, 1), (1, 0)),
    ((0, 0), (0, 1), (1, 0), (1, 1)),
    ((0, 0), (0, 1), (1, 0), (1, 1)),
    ((0, 0), (0, 1), (1, 1)),
    ((0, 0), (1, 0), (1, 1)),
)
COUNTS = tuple(len(p) for p in PAIRS)
RIM_OF = (0, 1, 2, 3, 0, 0, 1, 1)


def place(half, tile, part):
    return 4 * half + 2 * tile + part


def lanes_of(part):
    return slice(part * 128, part * 128 + 128)


def put_row(grid, pitch, tile, row, first, value):
    count = value.shape[0]
    for half in range(2):
        i = row - HALF * half
        if 0 <= i < TALL:
            for part in range(2):
                at = (i * pitch + first) * 8 + place(half, tile, part)
                grid[pl.ds(at, count, stride=8), :] = value[:, lanes_of(part)]


def put_column(grid, tile, col, value):
    for half in range(2):
        lo = max(0, HALF * half - RIM)
        hi = min(SIZE, HALF * half + HALF + RIM)
        for part in range(2):
            at = ((lo + RIM - HALF * half) * WIDE + col) * 8 + place(half, tile, part)
            grid[pl.ds(at, hi - lo, stride=WIDE * 8), :] = value[lo:hi, lanes_of(part)]


def fetch_strips(near_ids, own, slots, strips, near):
    def fetch(p, carry):
        t, d = p // 8, p % 8
        slot = near_ids[t, d]
        other = slot // 2
        s = slot - 2 * other
        off = lax.rem(other - own + slots // 2 + slots // 4, slots // 2) - slots // 4
        off = jnp.where(slot < 0, slots, off)

        @pl.when(slot < 0)
        def _():
            near[p] = jnp.zeros((RIM, SIZE, CH), F32)

        for strip, offset in zip(strips, OFFSETS):
            index = s if offset == 0 else 2 * s + t if abs(offset) == 1 else s + t

            @pl.when(off == offset)
            def _(strip=strip, index=index):
                near[p] = strip[index].astype(F32)

        return carry

    lax.fori_loop(0, 16, fetch, 0)


def put_halo(near, grid):
    for t in range(2):
        for i in range(RIM):
            for row, mid, west, east in ((i, 0, 4, 5), (RIM + SIZE + i, 1, 6, 7)):
                put_row(grid, WIDE, t, row, 0, near[t * 8 + west, i, SIZE - RIM : SIZE, :])
                put_row(grid, WIDE, t, row, RIM, near[t * 8 + mid, i])
                put_row(grid, WIDE, t, row, RIM + SIZE, near[t * 8 + east, i, 0:RIM, :])
        for k in range(RIM):
            put_column(grid, t, k, near[t * 8 + 2, k])
            put_column(grid, t, RIM + SIZE + k, near[t * 8 + 3, k])


def pick_rim(near_ids, own, slots, s, offset, t):
    slot = lax.rem(2 * own + 2 * offset + t + slots, slots)
    rim = jnp.int32(0)
    for d in range(8):
        rim = jnp.where(near_ids[s, d] == slot, RIM_OF[d], rim)
    return 4 * s + rim


def send_strips(near_ids, own, slots, rims, outs):
    for out, offset, pairs in zip(outs, OFFSETS, PAIRS):
        for k, (s, t) in enumerate(pairs):
            out[k] = rims[pick_rim(near_ids, own, slots, s, offset, t)]


def spread_taps(kernel_ref, taps):
    even = lax.rem(lax.broadcasted_iota(jnp.int32, (8, 128), 0), 2) == 0
    for q in range(TAPS):
        low = jnp.broadcast_to(kernel_ref[q : q + 1, 0:128], (8, 128))
        high = jnp.broadcast_to(kernel_ref[q : q + 1, 128:256], (8, 128))
        taps[q] = jnp.where(even, low, high)


def convolve(grid3, taps, flip, out3):
    def column(j, carry):
        acc = [None] * HALF
        for b in range(KW):
            cells = [grid3[i * WIDE + j + b] for i in range(TALL)]
            for a in range(KW):
                q = a * KW + b
                tap = taps[TAPS - 1 - q if flip else q]
                for r in range(HALF):
                    term = cells[r + a] * tap
                    acc[r] = term if acc[r] is None else acc[r] + term
        for r in range(HALF):
            out3[r * SIZE + j] = acc[r]
        return carry

    lax.fori_loop(0, SIZE, column, 0)


def rows_of(flat, tile, half, r):
    return jnp.concatenate(
        [flat[pl.ds(r * SIZE * 8 + place(half, tile, part), SIZE, stride=8), :] for part in range(2)], axis=1
    )


def gelu_parts(x):
    size = jnp.abs(x)
    t = pl.reciprocal(1.0 + (0.3275911 * 0.7071067811865476) * size, approx=False)
    bell = jnp.exp2((-0.5 * 1.4426950408889634) * (x * x))
    poly = 0.5 * 1.061405429 * t - 0.5 * 1.453152027
    poly = poly * t + 0.5 * 1.421413741
    poly = poly * t - 0.5 * 0.284496736
    poly = poly * t + 0.5 * 0.254829592
    tail = poly * t * bell
    cdf = jnp.where(x < 0, tail, 1.0 - tail)
    return x * cdf, cdf + x * (bell * 0.3989422804014327)


def rim_kernel(own_ref, near_ids, tile_ref, *rest, slots):
    outs, (rims, stage) = rest[:5], rest[5:]
    for s in range(2):
        rims[4 * s] = tile_ref[s, 0:RIM]
        rims[4 * s + 1] = tile_ref[s, SIZE - RIM : SIZE]
        for side, first, row in ((2, 0, 0), (3, 16, 16 - RIM)):
            for part in range(2):
                stage[part] = tile_ref[s, :, first : first + 16, lanes_of(part)].astype(F32).reshape(SIZE * 16, 128)
                for k in range(RIM):
                    rims[4 * s + side, k, :, lanes_of(part)] = stage[part, pl.ds(row + k, SIZE, stride=16), :].astype(BF16)
    send_strips(near_ids, own_ref[0], slots, rims, outs)


def grid_kernel(tile_ref, grid):
    for t in range(2):
        for i in range(SIZE):
            put_row(grid, WIDE, t, RIM + i, RIM, tile_ref[t, i].astype(F32))


def main_kernel(own_ref, near_ids, s0, s1, s2, s3, s4, kernel_ref, gain_ref, w_in_ref, w_out_ref, cot_ref, grid_in,
                gw_ref, grad_grid, o0, o1, o2, o3, o4, ggain_ref, grid,
                near, taps, conv, gwi, gwo, rims, *, slots):
    own = own_ref[0]
    grid[...] = grid_in[...]
    fetch_strips(near_ids, own, slots, (s0, s1, s2, s3, s4), near)
    put_halo(near, grid)
    spread_taps(kernel_ref, taps)
    convolve(grid.reshape(TALL * WIDE, 8, 128), taps, False, conv.reshape(HALF * SIZE, 8, 128))
    gwi[...] = jnp.zeros_like(gwi)
    gwo[...] = jnp.zeros_like(gwo)
    ggain_ref[...] = jnp.zeros_like(ggain_ref)
    gain = gain_ref[...]
    lines = ROWS // SIZE

    def chunk(n, carry):
        tile, half, first = n // 4, (n // 2) % 2, (n % 2) * lines
        spot = place(half, tile, 0)
        cv = jnp.concatenate(
            [
                jnp.concatenate(
                    [conv[pl.ds((first + r) * SIZE * 8 + spot + part, SIZE, stride=8), :] for part in range(2)], axis=1
                )
                for r in range(lines)
            ],
            axis=0,
        )
        mean = jnp.mean(cv, axis=-1, keepdims=True)
        cv = cv - mean
        inv = lax.rsqrt(jnp.mean(cv * cv, axis=-1, keepdims=True) + 1e-06)
        xhat = cv * inv
        normed = (xhat * gain).astype(BF16)
        cot = cot_ref[pl.ds(pl.multiple_of(n * ROWS, ROWS), ROWS), :]
        normed_t = normed.T
        cot_t = cot.T
        gn = jnp.zeros((ROWS, CH), F32)
        for f in range(FF // 256):
            cols = slice(f * 256, f * 256 + 256)
            pre = jnp.dot(normed, w_in_ref[:, cols], preferred_element_type=F32)
            gact = lax.dot_general(cot, w_out_ref[cols, :], (((1,), (1,)), ((), ())), preferred_element_type=F32)
            act, slope = gelu_parts(pre)
            act = act.astype(BF16)
            gpre = (gact * slope).astype(BF16)
            gwi[:, cols] += jnp.dot(normed_t, gpre, preferred_element_type=F32)
            gwo[:, cols] += jnp.dot(cot_t, act, preferred_element_type=F32)
            gn += lax.dot_general(gpre, w_in_ref[:, cols], (((1,), (1,)), ((), ())), preferred_element_type=F32)
        ggain_ref[...] += jnp.sum((gn * xhat).reshape(ROWS // 8, 8, CH), axis=0)
        gx = gn * gain
        m1 = jnp.mean(gx, axis=-1, keepdims=True)
        m2 = jnp.mean(gx * xhat, axis=-1, keepdims=True)
        gc = (inv * (gx - m1 - xhat * m2)).astype(BF16).astype(F32)
        for r in range(lines):
            piece = gc[r * SIZE : (r + 1) * SIZE]
            at = ((first + r + RIM) * WIDE + RIM) * 8 + spot
            for part in range(2):
                grad_grid[pl.ds(at + part, SIZE, stride=8), :] = piece[:, lanes_of(part)]
        return carry

    lax.fori_loop(0, 2 * SIZE * SIZE // ROWS, chunk, 0)
    low = lax.broadcasted_iota(jnp.int32, (CH, 128), 1) < 64
    for p in range(FF // 128):
        one = gwi[:, p * 128 : p * 128 + 128]
        two = gwo[:, p * 128 : p * 128 + 128]
        gw_ref[2 * p] = jnp.where(low, one, pltpu.roll(two, 64, 1)).astype(BF16)
        gw_ref[2 * p + 1] = jnp.where(low, pltpu.roll(one, 64, 1), two).astype(BF16)
    for t in range(2):
        for part in range(2):
            for r in range(RIM):
                for half, at, other in ((0, RIM + HALF + r, RIM + r), (1, r, HALF + r)):
                    mine = ((at * WIDE) + RIM) * 8 + place(half, t, part)
                    theirs = ((other * WIDE) + RIM) * 8 + place(1 - half, t, part)
                    grad_grid[pl.ds(mine, SIZE, stride=8), :] = grad_grid[pl.ds(theirs, SIZE, stride=8), :]
            lanes = lanes_of(part)
            for k in range(RIM):
                top = ((RIM + k) * WIDE + RIM) * 8 + place(0, t, part)
                bottom = ((HALF + k) * WIDE + RIM) * 8 + place(1, t, part)
                rims[4 * t, k, :, lanes] = grad_grid[pl.ds(top, SIZE, stride=8), :].astype(BF16)
                rims[4 * t + 1, k, :, lanes] = grad_grid[pl.ds(bottom, SIZE, stride=8), :].astype(BF16)
                for side, col in ((2, RIM + k), (3, SIZE + k)):
                    both = [
                        grad_grid[pl.ds((RIM * WIDE + col) * 8 + place(half, t, part), HALF, stride=WIDE * 8), :]
                        for half in range(2)
                    ]
                    rims[4 * t + side, k, :, lanes] = jnp.concatenate(both, axis=0).astype(BF16)
    send_strips(near_ids, own, slots, rims, (o0, o1, o2, o3, o4))


def taps_kernel(grid, grad_grid, ggain_ref, out_ref, acc):
    grid3 = grid.reshape(TALL * WIDE, 8, 128)
    grad3 = grad_grid.reshape(TALL * WIDE, 8, 128)
    acc[...] = jnp.zeros_like(acc)

    def column(j, carry):
        g = [grad3[(RIM + r) * WIDE + RIM + j] for r in range(HALF)]
        for b in range(KW):
            cells = [grid3[i * WIDE + j + b] for i in range(TALL)]
            for a in range(KW):
                terms = [cells[r + a] * g[r] for r in range(HALF)]
                while len(terms) > 1:
                    terms = [terms[k] + terms[k + 1] for k in range(0, len(terms), 2)]
                acc[a * KW + b] += terms[0]
        return carry

    lax.fori_loop(0, SIZE, column, 0)
    sub = lax.broadcasted_iota(jnp.int32, (8, 128), 0)
    even = lax.rem(sub, 2) == 0
    sums = [[], []]
    for q in range(TAPS):
        one = acc[q]
        sums[0].append(jnp.sum(jnp.where(even, one, 0.0), axis=0, keepdims=True))
        sums[1].append(jnp.sum(jnp.where(even, 0.0, one), axis=0, keepdims=True))
    for part in range(2):
        sums[part].append(jnp.sum(ggain_ref[:, lanes_of(part)], axis=0, keepdims=True))
        sums[part].append(jnp.zeros((64 - TAPS - 1, 128), F32))
    total = jnp.concatenate(sums[0] + sums[1], axis=0).astype(BF16)
    for d in range(16):
        out_ref[d] = total


def back_kernel(own_ref, near_ids, s0, s1, s2, s3, s4, kernel_ref, cot_ref, grid_in, out_ref, grid, near, taps, conv, *, slots):
    grid[...] = grid_in[...]
    fetch_strips(near_ids, own_ref[0], slots, (s0, s1, s2, s3, s4), near)
    put_halo(near, grid)
    spread_taps(kernel_ref, taps)
    convolve(grid.reshape(TALL * WIDE, 8, 128), taps, True, conv.reshape(HALF * SIZE, 8, 128))
    for t in range(2):
        for i in range(SIZE):
            out_ref[t, i] = (cot_ref[t, i].astype(F32) + rows_of(conv, t, i // HALF, i % HALF)).astype(BF16)


def first_sum_kernel(w_ref, k_ref, out_ref, low, stage):
    low[...] = jnp.sum(k_ref[...].astype(F32), axis=0)
    weights = jnp.sum(w_ref[...].astype(F32), axis=0)
    stage[...] = jnp.zeros_like(stage)
    for p in range(32):
        stage[p, 0:8, :] = weights[8 * p : 8 * p + 8]
        stage[p, 8:12, :] = low[4 * p : 4 * p + 4, :]
    out_ref[...] = stage[...].astype(BF16)


def second_sum_kernel(in_ref, out_ref):
    total = jnp.sum(in_ref[...].astype(F32), axis=0).astype(BF16)
    for p in range(32):
        out_ref[p] = total


def last_kernel(in_ref, w_in_ref, w_out_ref, taps_ref, gain_ref, stage, low, *, scale):
    stage[...] = in_ref[...].astype(F32) * scale
    weights = stage[:, 0:8, :].reshape(CH, 128)
    w_in_ref[...] = weights[:, 0:64]
    w_out_ref[...] = weights.T[64:128, :]
    for p in range(32):
        low[4 * p : 4 * p + 4, :] = stage[p, 8:12, :]
    for part in range(2):
        lanes = lanes_of(part)
        taps_ref[:, lanes] = low[64 * part : 64 * part + TAPS, :]
        gain_ref[:, lanes] = low[64 * part + TAPS : 64 * part + TAPS + 1, :]


SMEM = pl.BlockSpec(memory_space=pltpu.SMEM)
STRIPS = tuple(jax.ShapeDtypeStruct((n, RIM, SIZE, CH), BF16) for n in COUNTS)
RIMS = pltpu.VMEM((8, RIM, SIZE, CH), BF16)
NEAR = pltpu.VMEM((16, RIM, SIZE, CH), F32)
GRID = jax.ShapeDtypeStruct((TALL * WIDE * 8, 128), F32)
GRID_SPACE = pltpu.VMEM(GRID.shape, F32)
SPREAD = pltpu.VMEM((TAPS, 8, 128), F32)
CONV = pltpu.VMEM((HALF * SIZE * 8, 128), F32)


def call(kernel, name, out, scalars, arrays, scratch=(), flops=10**6, moved=10**6):
    vmem = pl.BlockSpec(memory_space=pltpu.VMEM)
    many = isinstance(out, tuple)
    return pl.pallas_call(
        kernel,
        out_shape=out,
        in_specs=[SMEM] * len(scalars) + [vmem] * len(arrays),
        out_specs=[vmem] * len(out) if many else vmem,
        scratch_shapes=scratch,
        compiler_params=pltpu.CompilerParams(vmem_limit_bytes=VMEM_LIMIT),
        cost_estimate=pl.CostEstimate(flops=flops, bytes_accessed=moved, transcendentals=0),
        name=name,
    )(*scalars, *arrays)


def exchange(strips):
    n = lax.axis_size("tiles")
    got = {0: strips[0]}
    for off, strip in zip(OFFSETS[1:], strips[1:]):
        got[-off] = lax.ppermute(strip, "tiles", [(i, (i + off) % n) for i in range(n)])
    return tuple(got[off] for off in OFFSETS)


def body(fields, neighbours, kernel, gain, w_in, w_out, cotangent):
    n_tiles, n_dp = lax.axis_size("tiles"), lax.axis_size("dp")
    slots = 2 * n_tiles
    scalars = (lax.axis_index("tiles").reshape(1).astype(jnp.int32), neighbours)
    taps = kernel.reshape(TAPS, CH)
    tiles, cot = fields[0], cotangent[0]
    stage = pltpu.VMEM((2, SIZE * 16, 128), F32)
    sent = call(functools.partial(rim_kernel, slots=slots), "rims", STRIPS, scalars, (tiles,), (RIMS, stage))
    grid = call(grid_kernel, "grid", GRID, (), (tiles,), moved=5 * 10**6)
    got = exchange(sent)
    outs = (jax.ShapeDtypeStruct((16, CH, 128), BF16), GRID, *STRIPS, jax.ShapeDtypeStruct((8, CH), F32), GRID)
    weights, grad_grid, *rest = call(
        functools.partial(main_kernel, slots=slots),
        "main",
        outs,
        scalars,
        (*got, taps, gain.reshape(1, CH), w_in, w_out, cot.reshape(-1, CH), grid),
        (NEAR, SPREAD, CONV, pltpu.VMEM((CH, FF), F32), pltpu.VMEM((CH, FF), F32), RIMS),
        flops=20 * 10**9,
    )
    sent, ggain, grid = rest[:5], rest[5], rest[6]
    weights = lax.all_to_all(weights, "dp", 0, 0, tiled=True)
    small = call(
        taps_kernel,
        "taps",
        jax.ShapeDtypeStruct((16, 128, 128), BF16),
        (),
        (grid, grad_grid, ggain),
        (pltpu.VMEM((TAPS, 8, 128), F32),),
        flops=8 * 10**9,
    )
    small = lax.all_to_all(small, "dp", 0, 0, tiled=True)
    got = exchange(sent)
    grad_fields = call(
        functools.partial(back_kernel, slots=slots),
        "back",
        jax.ShapeDtypeStruct((2, SIZE, SIZE, CH), BF16),
        scalars,
        (*got, taps, cot, grad_grid),
        (GRID_SPACE, NEAR, SPREAD, CONV),
        flops=8 * 10**9,
    )
    pieces = jax.ShapeDtypeStruct((32, 16, 128), BF16)
    stages = (pltpu.VMEM((128, 128), F32), pltpu.VMEM((32, 16, 128), F32))
    cut = call(first_sum_kernel, "sum_dp", pieces, (), (weights, small), stages)
    cut = lax.all_to_all(cut, "tiles", 0, 0, tiled=True)
    cut = call(second_sum_kernel, "sum_tiles", pieces, (), (cut,))
    cut = lax.all_to_all(cut, "tiles", 0, 0, tiled=True)
    scale = float((n_dp * slots * SIZE * SIZE) ** -0.5)
    g_in, g_out, g_taps, g_gain = call(
        functools.partial(last_kernel, scale=scale),
        "last",
        (
            jax.ShapeDtypeStruct((CH, 64), F32),
            jax.ShapeDtypeStruct((64, CH), F32),
            jax.ShapeDtypeStruct((TAPS, CH), F32),
            jax.ShapeDtypeStruct((1, CH), F32),
        ),
        (),
        (cut,),
        (stages[1], stages[0]),
    )
    return grad_fields[None], g_in, g_out, g_taps.reshape(KW, KW, CH), g_gain.reshape(CH)


def solution(mesh):
    return jax.shard_map(
        body,
        mesh=mesh,
        in_specs=(
            P("dp", "tiles", None, None, None),
            P("tiles", None),
            P(),
            P(),
            P(),
            P(),
            P("dp", "tiles", None, None, None),
        ),
        out_specs=(P("dp", "tiles", None, None, None), P(None, "dp"), P("dp", None), P(), P()),
        check_vma=False,
    )
```

```python
import functools

import jax
import jax.numpy as jnp
from jax import lax
from jax.experimental import pallas as pl
from jax.experimental.pallas import tpu as pltpu
from jax.sharding import PartitionSpec as P

KW = 7
TAPS = KW * KW
RIM = KW // 2
SIZE = 32
WIDE = SIZE + 2 * RIM
HALF = SIZE // 2
TALL = HALF + 2 * RIM
CH = 256
FF = 1024
PART_ROWS = 56
ROWS = 256
F32 = jnp.float32
BF16 = jnp.bfloat16
OFFSETS = (0, -1, 1, -2, 2)
PAIRS = (
    ((0, 1), (1, 0)),
    ((0, 0), (0, 1), (1, 0), (1, 1)),
    ((0, 0), (0, 1), (1, 0), (1, 1)),
    ((0, 0), (0, 1), (1, 1)),
    ((0, 0), (1, 0), (1, 1)),
)
COUNTS = tuple(len(p) for p in PAIRS)
RIM_OF = (0, 1, 2, 3, 0, 0, 1, 1)


def place(half, tile, part):
    return 4 * half + 2 * tile + part


def lanes_of(part):
    return slice(part * 128, part * 128 + 128)


def put_row(grid, pitch, tile, row, first, value):
    count = value.shape[0]
    for half in range(2):
        i = row - HALF * half
        if 0 <= i < TALL:
            for part in range(2):
                at = (i * pitch + first) * 8 + place(half, tile, part)
                grid[pl.ds(at, count, stride=8), :] = value[:, lanes_of(part)]


def put_column(grid, tile, col, value):
    for half in range(2):
        lo = max(0, HALF * half - RIM)
        hi = min(SIZE, HALF * half + HALF + RIM)
        for part in range(2):
            at = ((lo + RIM - HALF * half) * WIDE + col) * 8 + place(half, tile, part)
            grid[pl.ds(at, hi - lo, stride=WIDE * 8), :] = value[lo:hi, lanes_of(part)]


def fetch_strips(near_ids, own, slots, strips, near):
    def fetch(p, carry):
        t, d = p // 8, p % 8
        slot = near_ids[t, d]
        other = slot // 2
        s = slot - 2 * other
        off = lax.rem(other - own + slots // 2 + slots // 4, slots // 2) - slots // 4
        off = jnp.where(slot < 0, slots, off)

        @pl.when(slot < 0)
        def _():
            near[p] = jnp.zeros((RIM, SIZE, CH), F32)

        for strip, offset in zip(strips, OFFSETS):
            index = s if offset == 0 else 2 * s + t if abs(offset) == 1 else s + t

            @pl.when(off == offset)
            def _(strip=strip, index=index):
                near[p] = strip[index].astype(F32)

        return carry

    lax.fori_loop(0, 16, fetch, 0)


def put_halo(near, grid):
    for t in range(2):
        for i in range(RIM):
            for row, mid, west, east in ((i, 0, 4, 5), (RIM + SIZE + i, 1, 6, 7)):
                put_row(grid, WIDE, t, row, 0, near[t * 8 + west, i, SIZE - RIM : SIZE, :])
                put_row(grid, WIDE, t, row, RIM, near[t * 8 + mid, i])
                put_row(grid, WIDE, t, row, RIM + SIZE, near[t * 8 + east, i, 0:RIM, :])
        for k in range(RIM):
            put_column(grid, t, k, near[t * 8 + 2, k])
            put_column(grid, t, RIM + SIZE + k, near[t * 8 + 3, k])


def pick_rim(near_ids, own, slots, s, offset, t):
    slot = lax.rem(2 * own + 2 * offset + t + slots, slots)
    rim = jnp.int32(0)
    for d in range(8):
        rim = jnp.where(near_ids[s, d] == slot, RIM_OF[d], rim)
    return 4 * s + rim


def send_strips(near_ids, own, slots, rims, outs):
    for out, offset, pairs in zip(outs, OFFSETS, PAIRS):
        for k, (s, t) in enumerate(pairs):
            out[k] = rims[pick_rim(near_ids, own, slots, s, offset, t)]


def spread_taps(kernel_ref, taps):
    even = lax.rem(lax.broadcasted_iota(jnp.int32, (8, 128), 0), 2) == 0
    for a in range(KW):
        for b in range(KW):
            low = jnp.broadcast_to(kernel_ref[a, b : b + 1, 0:128], (8, 128))
            high = jnp.broadcast_to(kernel_ref[a, b : b + 1, 128:256], (8, 128))
            taps[a * KW + b] = jnp.where(even, low, high)


def convolve(grid3, taps, flip, out3):
    def column(j, carry):
        acc = [None] * HALF
        for q in range(TAPS):
            tap = taps[TAPS - 1 - q if flip else q]
            for r in range(HALF):
                term = grid3[(r + q // KW) * WIDE + j + q % KW] * tap
                acc[r] = term if acc[r] is None else acc[r] + term
        for r in range(HALF):
            out3[r * SIZE + j] = acc[r]
        return carry

    lax.fori_loop(0, SIZE, column, 0)


def rows_of(flat, tile, half, r):
    return jnp.concatenate(
        [flat[pl.ds(r * SIZE * 8 + place(half, tile, part), SIZE, stride=8), :] for part in range(2)], axis=1
    )


def gelu_parts(x):
    size = jnp.abs(x)
    t = pl.reciprocal(1.0 + (0.3275911 * 0.7071067811865476) * size, approx=False)
    bell = jnp.exp2((-0.5 * 1.4426950408889634) * (x * x))
    poly = 0.5 * 1.061405429 * t - 0.5 * 1.453152027
    poly = poly * t + 0.5 * 1.421413741
    poly = poly * t - 0.5 * 0.284496736
    poly = poly * t + 0.5 * 0.254829592
    tail = poly * t * bell
    cdf = jnp.where(x < 0, tail, 1.0 - tail)
    return x * cdf, cdf + x * (bell * 0.3989422804014327)


def rim_kernel(own_ref, near_ids, tile_ref, *rest, slots):
    outs, (rims, stage) = rest[:5], rest[5:]
    for s in range(2):
        rims[4 * s] = tile_ref[s, 0:RIM]
        rims[4 * s + 1] = tile_ref[s, SIZE - RIM : SIZE]
        for side, first, row in ((2, 0, 0), (3, 16, 16 - RIM)):
            for part in range(2):
                stage[part] = tile_ref[s, :, first : first + 16, lanes_of(part)].astype(F32).reshape(SIZE * 16, 128)
                for k in range(RIM):
                    rims[4 * s + side, k, :, lanes_of(part)] = stage[part, pl.ds(row + k, SIZE, stride=16), :].astype(BF16)
    send_strips(near_ids, own_ref[0], slots, rims, outs)


def grid_kernel(tile_ref, grid):
    for t in range(2):
        for i in range(SIZE):
            put_row(grid, WIDE, t, RIM + i, RIM, tile_ref[t, i].astype(F32))


def main_kernel(own_ref, near_ids, s0, s1, s2, s3, s4, kernel_ref, gain_ref, w_in_hbm, w_out_hbm, cot_hbm, grid_hbm,
                share_ref, grad_grid, o0, o1, o2, o3, o4,
                grid, near, taps, conv, gwi, gwo, rims, normed_ref, xhat_ref, inv_ref, gn_ref,
                cot_ref, w_in_ref, w_out_ref, acc, sems, *, slots):
    own = own_ref[0]
    copies = [
        pltpu.make_async_copy(src, dst, sems.at[k])
        for k, (src, dst) in enumerate(
            ((grid_hbm, grid), (w_in_hbm, w_in_ref), (w_out_hbm, w_out_ref), (cot_hbm, cot_ref))
        )
    ]
    for copy in copies:
        copy.start()
    fetch_strips(near_ids, own, slots, (s0, s1, s2, s3, s4), near)
    spread_taps(kernel_ref, taps)
    copies[0].wait()
    put_halo(near, grid)
    grid3 = grid.reshape(TALL * WIDE, 8, 128)
    convolve(grid3, taps, False, conv.reshape(HALF * SIZE, 8, 128))
    gain = gain_ref[...]
    lines = ROWS // SIZE

    def where(n):
        return (n % 2) * lines, place((n // 2) % 2, n // 4, 0)

    def normalise(n, carry):
        first, spot = where(n)
        cells = pl.ds(pl.multiple_of(n * ROWS, ROWS), ROWS)
        cv = jnp.concatenate(
            [
                jnp.concatenate(
                    [conv[pl.ds((first + r) * SIZE * 8 + spot + part, SIZE, stride=8), :] for part in range(2)], axis=1
                )
                for r in range(lines)
            ],
            axis=0,
        )
        cv = cv - jnp.mean(cv, axis=-1, keepdims=True)
        inv = lax.rsqrt(jnp.mean(cv * cv, axis=-1, keepdims=True) + 1e-06)
        xhat = cv * inv
        xhat_ref[cells, :] = xhat
        inv_ref[cells, :] = jnp.broadcast_to(inv, (ROWS, 128))
        normed_ref[cells, :] = (xhat * gain).astype(BF16)
        return carry

    lax.fori_loop(0, 2 * SIZE * SIZE // ROWS, normalise, 0)
    for copy in copies[1:]:
        copy.wait()
    steps = [(t, slice(f * 256, f * 256 + 256)) for t in range(2) for f in range(FF // 256)]
    cells_of = [slice(t * SIZE * SIZE, (t + 1) * SIZE * SIZE) for t in range(2)]
    across = (((1,), (1,)), ((), ()))

    def forward(step):
        t, cols = step
        pre = jnp.dot(normed_ref[cells_of[t], :], w_in_ref[:, cols], preferred_element_type=F32)
        return pre, lax.dot_general(cot_ref[cells_of[t], :], w_out_ref[cols, :], across, preferred_element_type=F32)

    ahead = forward(steps[0])
    for k, (t, cols) in enumerate(steps):
        pre, gact = ahead
        if k + 1 < len(steps):
            ahead = forward(steps[k + 1])
        if cols.start == 0:
            normed_t = normed_ref[cells_of[t], :].T
            cot_t = cot_ref[cells_of[t], :].T
        act, slope = gelu_parts(pre)
        act = act.astype(BF16)
        gpre = (gact * slope).astype(BF16)
        one = jnp.dot(normed_t, gpre, preferred_element_type=F32)
        two = jnp.dot(cot_t, act, preferred_element_type=F32)
        gn = lax.dot_general(gpre, w_in_ref[:, cols], across, preferred_element_type=F32)
        if t == 0:
            gwi[:, cols] = one
            gwo[:, cols] = two
        else:
            gwi[:, cols] += one
            gwo[:, cols] += two
        if cols.start == 0:
            gn_ref[cells_of[t], :] = gn
        else:
            gn_ref[cells_of[t], :] += gn

    def denormalise(n, ggain):
        first, spot = where(n)
        cells = pl.ds(pl.multiple_of(n * ROWS, ROWS), ROWS)
        gn, xhat = gn_ref[cells, :], xhat_ref[cells, :]
        inv = inv_ref[cells, 0:1]
        ggain = ggain + jnp.sum((gn * xhat).reshape(ROWS // 8, 8, CH), axis=0)
        gx = gn * gain
        m1 = jnp.mean(gx, axis=-1, keepdims=True)
        m2 = jnp.mean(gx * xhat, axis=-1, keepdims=True)
        gc = (inv * (gx - m1 - xhat * m2)).astype(BF16).astype(F32)
        for r in range(lines):
            piece = gc[r * SIZE : (r + 1) * SIZE]
            at = ((first + r + RIM) * WIDE + RIM) * 8 + spot
            for part in range(2):
                grad_grid[pl.ds(at + part, SIZE, stride=8), :] = piece[:, lanes_of(part)]
        return ggain

    ggain = lax.fori_loop(0, 2 * SIZE * SIZE // ROWS, denormalise, jnp.zeros((8, CH), F32))
    low = lax.broadcasted_iota(jnp.int32, (CH, 128), 1) < 64
    for p in range(FF // 128):
        one = gwi[:, p * 128 : p * 128 + 128]
        two = gwo[:, p * 128 : p * 128 + 128]
        share_ref[2 * p, 0:CH] = jnp.where(low, one, pltpu.roll(two, 64, 1)).astype(BF16)
        share_ref[2 * p + 1, 0:CH] = jnp.where(low, pltpu.roll(one, 64, 1), two).astype(BF16)
    tap_gradients(grid3, grad_grid.reshape(TALL * WIDE, 8, 128), ggain, acc, share_ref)
    for t in range(2):
        for part in range(2):
            for r in range(RIM):
                for half, at, other in ((0, RIM + HALF + r, RIM + r), (1, r, HALF + r)):
                    mine = ((at * WIDE) + RIM) * 8 + place(half, t, part)
                    theirs = ((other * WIDE) + RIM) * 8 + place(1 - half, t, part)
                    grad_grid[pl.ds(mine, SIZE, stride=8), :] = grad_grid[pl.ds(theirs, SIZE, stride=8), :]
            lanes = lanes_of(part)
            for k in range(RIM):
                top = ((RIM + k) * WIDE + RIM) * 8 + place(0, t, part)
                bottom = ((HALF + k) * WIDE + RIM) * 8 + place(1, t, part)
                rims[4 * t, k, :, lanes] = grad_grid[pl.ds(top, SIZE, stride=8), :].astype(BF16)
                rims[4 * t + 1, k, :, lanes] = grad_grid[pl.ds(bottom, SIZE, stride=8), :].astype(BF16)
                for side, col in ((2, RIM + k), (3, SIZE + k)):
                    both = [
                        grad_grid[pl.ds((RIM * WIDE + col) * 8 + place(half, t, part), HALF, stride=WIDE * 8), :]
                        for half in range(2)
                    ]
                    rims[4 * t + side, k, :, lanes] = jnp.concatenate(both, axis=0).astype(BF16)
    send_strips(near_ids, own, slots, rims, (o0, o1, o2, o3, o4))


def tap_gradients(grid3, grad3, ggain, acc, share_ref):
    acc[...] = jnp.zeros_like(acc)

    def column(j, carry):
        g = [grad3[(RIM + r) * WIDE + RIM + j] for r in range(HALF)]
        for q in range(TAPS):
            terms = [grid3[(r + q // KW) * WIDE + j + q % KW] * g[r] for r in range(HALF)]
            while len(terms) > 1:
                terms = [terms[k] + terms[k + 1] for k in range(0, len(terms), 2)]
            acc[q] += terms[0]
        return carry

    lax.fori_loop(0, SIZE, column, 0)
    even = lax.rem(lax.broadcasted_iota(jnp.int32, (8, 128), 0), 2) == 0
    sums = [[], []]
    for q in range(TAPS):
        one = acc[q]
        sums[0].append(jnp.sum(jnp.where(even, one, 0.0), axis=0, keepdims=True))
        sums[1].append(jnp.sum(jnp.where(even, 0.0, one), axis=0, keepdims=True))
    for part in range(2):
        sums[part].append(jnp.sum(ggain[:, lanes_of(part)], axis=0, keepdims=True))
        sums[part].append(jnp.zeros((PART_ROWS - TAPS - 1, 128), F32))
    total = jnp.concatenate(sums[0] + sums[1], axis=0).astype(BF16)
    for d in range(16):
        share_ref[d, CH : CH + 2 * PART_ROWS] = total


def back_kernel(own_ref, near_ids, s0, s1, s2, s3, s4, kernel_ref, cot_ref, grid_hbm, out_ref, grid, near, taps, conv, sem, *, slots):
    copy = pltpu.make_async_copy(grid_hbm, grid, sem)
    copy.start()
    fetch_strips(near_ids, own_ref[0], slots, (s0, s1, s2, s3, s4), near)
    spread_taps(kernel_ref, taps)
    copy.wait()
    put_halo(near, grid)
    convolve(grid.reshape(TALL * WIDE, 8, 128), taps, True, conv.reshape(HALF * SIZE, 8, 128))
    for t in range(2):
        for i in range(SIZE):
            out_ref[t, i] = (cot_ref[t, i].astype(F32) + rows_of(conv, t, i // HALF, i % HALF)).astype(BF16)


def first_sum_kernel(in_ref, out_ref, stage):
    weights = jnp.sum(in_ref[:, 0:CH, :].astype(F32), axis=0)
    small = jnp.sum(in_ref[:, CH : CH + 2 * PART_ROWS, :].astype(F32), axis=0)
    stage[...] = jnp.zeros_like(stage)
    for p in range(32):
        stage[p, 0:8, :] = weights[8 * p : 8 * p + 8]
        if 4 * p < 2 * PART_ROWS:
            stage[p, 8:12, :] = small[4 * p : 4 * p + 4]
    out_ref[...] = stage[...].astype(BF16)


def second_sum_kernel(in_ref, out_ref):
    total = jnp.sum(in_ref[...].astype(F32), axis=0).astype(BF16)
    for p in range(32):
        out_ref[p] = total


def last_kernel(in_ref, w_in_ref, w_out_ref, taps_ref, gain_ref, stage, low, *, scale):
    stage[...] = in_ref[...].astype(F32) * scale
    weights = stage[:, 0:8, :].reshape(CH, 128).T
    w_in_ref[...] = weights[0:64, :]
    w_out_ref[...] = weights[64:128, :]
    for p in range(PART_ROWS // 2):
        low[4 * p : 4 * p + 4, :] = stage[p, 8:12, :]
    for part in range(2):
        lanes = lanes_of(part)
        for a in range(KW):
            at = part * PART_ROWS + a * KW
            taps_ref[a, :, lanes] = low[at : at + KW, :]
        at = part * PART_ROWS + TAPS
        gain_ref[:, lanes] = low[at : at + 1, :]


SMEM = pl.BlockSpec(memory_space=pltpu.SMEM)
STRIPS = tuple(jax.ShapeDtypeStruct((n, RIM, SIZE, CH), BF16) for n in COUNTS)
RIMS = pltpu.VMEM((8, RIM, SIZE, CH), BF16)
NEAR = pltpu.VMEM((16, RIM, SIZE, CH), F32)
GRID = jax.ShapeDtypeStruct((TALL * WIDE * 8, 128), F32)
GRID_SPACE = pltpu.VMEM(GRID.shape, F32)
SPREAD = pltpu.VMEM((TAPS, 8, 128), F32)
CONV = pltpu.VMEM((HALF * SIZE * 8, 128), F32)


def call(kernel, name, out, scalars, arrays, scratch=(), far=(), flops=10**6, moved=10**6, vmem_mib=24):
    vmem = pl.BlockSpec(memory_space=pltpu.VMEM)
    anywhere = pl.BlockSpec(memory_space=pl.ANY)
    return pl.pallas_call(
        kernel,
        out_shape=out,
        in_specs=[SMEM] * len(scalars) + [vmem] * len(arrays) + [anywhere] * len(far),
        out_specs=[vmem] * len(out) if isinstance(out, tuple) else vmem,
        scratch_shapes=scratch,
        compiler_params=pltpu.CompilerParams(vmem_limit_bytes=vmem_mib * 1024 * 1024),
        cost_estimate=pl.CostEstimate(flops=flops, bytes_accessed=moved, transcendentals=0),
        name=name,
    )(*scalars, *arrays, *far)


def exchange(strips):
    n = lax.axis_size("tiles")
    got = {0: strips[0]}
    for off, strip in zip(OFFSETS[1:], strips[1:]):
        got[-off] = lax.ppermute(strip, "tiles", [(i, (i + off) % n) for i in range(n)])
    return tuple(got[off] for off in OFFSETS)


def body(fields, neighbours, kernel, gain, w_in, w_out, cotangent):
    n_tiles, n_dp = lax.axis_size("tiles"), lax.axis_size("dp")
    slots = 2 * n_tiles
    scalars = (lax.axis_index("tiles").reshape(1).astype(jnp.int32), neighbours)
    tiles, cot = fields[0], cotangent[0]
    stage = pltpu.VMEM((2, SIZE * 16, 128), F32)
    sent = call(functools.partial(rim_kernel, slots=slots), "rims", STRIPS, scalars, (tiles,), (RIMS, stage))
    grid = call(grid_kernel, "grid", GRID, (), (tiles,), moved=5 * 10**6)
    got = exchange(sent)
    cells = 2 * SIZE * SIZE
    share, grad_grid, *sent = call(
        functools.partial(main_kernel, slots=slots),
        "main",
        (jax.ShapeDtypeStruct((16, CH + 2 * PART_ROWS, 128), BF16), GRID, *STRIPS),
        scalars,
        (*got, kernel, gain.reshape(1, CH)),
        (
            GRID_SPACE, NEAR, SPREAD, CONV, pltpu.VMEM((CH, FF), F32), pltpu.VMEM((CH, FF), F32), RIMS,
            pltpu.VMEM((cells, CH), BF16), pltpu.VMEM((cells, CH), F32), pltpu.VMEM((cells, 128), F32),
            pltpu.VMEM((cells, CH), F32), pltpu.VMEM((cells, CH), BF16), pltpu.VMEM((CH, FF), BF16),
            pltpu.VMEM((FF, CH), BF16), pltpu.VMEM((TAPS, 8, 128), F32), pltpu.SemaphoreType.DMA((4,)),
        ),
        far=(w_in, w_out, cot.reshape(cells, CH), grid),
        flops=40 * 10**9,
        vmem_mib=48,
    )
    share = lax.all_to_all(share, "dp", 0, 0, tiled=True)
    got = exchange(sent)
    grad_fields = call(
        functools.partial(back_kernel, slots=slots),
        "back",
        jax.ShapeDtypeStruct((2, SIZE, SIZE, CH), BF16),
        scalars,
        (*got, kernel, cot),
        (GRID_SPACE, NEAR, SPREAD, CONV, pltpu.SemaphoreType.DMA(())),
        far=(grad_grid,),
        flops=12 * 10**9,
    )
    pieces = jax.ShapeDtypeStruct((32, 16, 128), BF16)
    stage = pltpu.VMEM((32, 16, 128), F32)
    cut = call(first_sum_kernel, "sum_dp", pieces, (), (share,), (stage,))
    cut = lax.all_to_all(cut, "tiles", 0, 0, tiled=True)
    cut = call(second_sum_kernel, "sum_tiles", pieces, (), (cut,))
    cut = lax.all_to_all(cut, "tiles", 0, 0, tiled=True)
    scale = float((n_dp * slots * SIZE * SIZE) ** -0.5)
    g_in, g_out, g_taps, g_gain = call(
        functools.partial(last_kernel, scale=scale),
        "last",
        (
            jax.ShapeDtypeStruct((64, CH), F32),
            jax.ShapeDtypeStruct((64, CH), F32),
            jax.ShapeDtypeStruct((KW, KW, CH), F32),
            jax.ShapeDtypeStruct((1, CH), F32),
        ),
        (),
        (cut,),
        (stage, pltpu.VMEM((2 * PART_ROWS, 128), F32)),
    )
    return grad_fields[None], g_in.T, g_out, g_taps, g_gain.reshape(CH)


def solution(mesh):
    return jax.shard_map(
        body,
        mesh=mesh,
        in_specs=(
            P("dp", "tiles", None, None, None),
            P("tiles", None),
            P(),
            P(),
            P(),
            P(),
            P("dp", "tiles", None, None, None),
        ),
        out_specs=(P("dp", "tiles", None, None, None), P(None, "dp"), P("dp", None), P(), P()),
        check_vma=False,
    )
```

```python
import functools

import jax
import jax.numpy as jnp
from jax import lax
from jax.experimental import pallas as pl
from jax.experimental.pallas import tpu as pltpu
from jax.sharding import PartitionSpec as P

KW = 7
TAPS = KW * KW
RIM = KW // 2
SIZE = 32
WIDE = SIZE + 2 * RIM
HALF = SIZE // 2
TALL = HALF + 2 * RIM
CH = 256
FF = 1024
NEAR_GROUP = 8
PIECE = 48
PART_ROWS = 64
ROWS = 256
F32 = jnp.float32
BF16 = jnp.bfloat16
OFFSETS = (0, -1, 1, -2, 2)
PAIRS = (
    ((0, 1), (1, 0)),
    ((0, 0), (0, 1), (1, 0), (1, 1)),
    ((0, 0), (0, 1), (1, 0), (1, 1)),
    ((0, 0), (0, 1), (1, 1)),
    ((0, 0), (1, 0), (1, 1)),
)
COUNTS = tuple(len(p) for p in PAIRS)
RIM_OF = (0, 1, 2, 3, 0, 0, 1, 1)


def place(half, tile, part):
    return 4 * half + 2 * tile + part


def lanes_of(part):
    return slice(part * 128, part * 128 + 128)


def put_row(grid, pitch, tile, row, first, value):
    count = value.shape[0]
    for half in range(2):
        i = row - HALF * half
        if 0 <= i < TALL:
            for part in range(2):
                at = (i * pitch + first) * 8 + place(half, tile, part)
                grid[pl.ds(at, count, stride=8), :] = value[:, lanes_of(part)]


def put_column(grid, tile, col, value):
    for half in range(2):
        lo = max(0, HALF * half - RIM)
        hi = min(SIZE, HALF * half + HALF + RIM)
        for part in range(2):
            at = ((lo + RIM - HALF * half) * WIDE + col) * 8 + place(half, tile, part)
            grid[pl.ds(at, hi - lo, stride=WIDE * 8), :] = value[lo:hi, lanes_of(part)]


def fetch_strips(near_ids, own, slots, strips, near):
    def fetch(p, carry):
        t, d = p // 8, p % 8
        slot = near_ids[t, d]
        other = slot // 2
        s = slot - 2 * other
        off = lax.rem(other - own + slots // 2 + slots // 4, slots // 2) - slots // 4
        off = jnp.where(slot < 0, slots, off)

        @pl.when(slot < 0)
        def _():
            near[p] = jnp.zeros((RIM, SIZE, CH), F32)

        for strip, offset in zip(strips, OFFSETS):
            index = s if offset == 0 else 2 * s + t if abs(offset) == 1 else s + t

            @pl.when(off == offset)
            def _(strip=strip, index=index):
                near[p] = strip[index].astype(F32)

        return carry

    lax.fori_loop(0, 16, fetch, 0)


def put_halo(near, grid):
    for t in range(2):
        for i in range(RIM):
            for row, mid, west, east in ((i, 0, 4, 5), (RIM + SIZE + i, 1, 6, 7)):
                put_row(grid, WIDE, t, row, 0, near[t * 8 + west, i, SIZE - RIM : SIZE, :])
                put_row(grid, WIDE, t, row, RIM, near[t * 8 + mid, i])
                put_row(grid, WIDE, t, row, RIM + SIZE, near[t * 8 + east, i, 0:RIM, :])
        for k in range(RIM):
            put_column(grid, t, k, near[t * 8 + 2, k])
            put_column(grid, t, RIM + SIZE + k, near[t * 8 + 3, k])


def pick_rim(near_ids, own, slots, s, offset, t):
    slot = lax.rem(2 * own + 2 * offset + t + slots, slots)
    rim = jnp.int32(0)
    for d in range(8):
        rim = jnp.where(near_ids[s, d] == slot, RIM_OF[d], rim)
    return 4 * s + rim


def send_strips(near_ids, own, slots, rims, outs):
    for out, offset, pairs in zip(outs, OFFSETS, PAIRS):
        for k, (s, t) in enumerate(pairs):
            out[k] = rims[pick_rim(near_ids, own, slots, s, offset, t)]


def spread_taps(kernel_ref, taps):
    even = lax.rem(lax.broadcasted_iota(jnp.int32, (8, 128), 0), 2) == 0
    for a in range(KW):
        for b in range(KW):
            low = jnp.broadcast_to(kernel_ref[a, b : b + 1, 0:128], (8, 128))
            high = jnp.broadcast_to(kernel_ref[a, b : b + 1, 128:256], (8, 128))
            taps[a * KW + b] = jnp.where(even, low, high)


def convolve(grid3, taps, flip, out3):
    def column(j, carry):
        acc = [None] * HALF
        for q in range(TAPS):
            tap = taps[TAPS - 1 - q if flip else q]
            for r in range(HALF):
                term = grid3[(r + q // KW) * WIDE + j + q % KW] * tap
                acc[r] = term if acc[r] is None else acc[r] + term
        for r in range(HALF):
            out3[r * SIZE + j] = acc[r]
        return carry

    lax.fori_loop(0, SIZE, column, 0)


def rows_of(flat, tile, half, r):
    return jnp.concatenate(
        [flat[pl.ds(r * SIZE * 8 + place(half, tile, part), SIZE, stride=8), :] for part in range(2)], axis=1
    )


def gelu_parts(x):
    size = jnp.abs(x)
    t = pl.reciprocal(1.0 + (0.3275911 * 0.7071067811865476) * size, approx=False)
    bell = jnp.exp2((-0.5 * 1.4426950408889634) * (x * x))
    poly = 0.5 * 1.061405429 * t - 0.5 * 1.453152027
    poly = poly * t + 0.5 * 1.421413741
    poly = poly * t - 0.5 * 0.284496736
    poly = poly * t + 0.5 * 0.254829592
    tail = poly * t * bell
    cdf = jnp.where(x < 0, tail, 1.0 - tail)
    return x * cdf, cdf + x * (bell * 0.3989422804014327)


def rim_kernel(own_ref, near_ids, tile_ref, *rest, slots):
    outs, (rims, stage) = rest[:5], rest[5:]
    for s in range(2):
        rims[4 * s] = tile_ref[s, 0:RIM]
        rims[4 * s + 1] = tile_ref[s, SIZE - RIM : SIZE]
        for side, first, row in ((2, 0, 0), (3, 16, 16 - RIM)):
            for part in range(2):
                stage[part] = tile_ref[s, :, first : first + 16, lanes_of(part)].astype(F32).reshape(SIZE * 16, 128)
                for k in range(RIM):
                    rims[4 * s + side, k, :, lanes_of(part)] = stage[part, pl.ds(row + k, SIZE, stride=16), :].astype(BF16)
    send_strips(near_ids, own_ref[0], slots, rims, outs)


def grid_kernel(tile_ref, grid):
    for t in range(2):
        for i in range(SIZE):
            put_row(grid, WIDE, t, RIM + i, RIM, tile_ref[t, i].astype(F32))


def main_kernel(own_ref, near_ids, s0, s1, s2, s3, s4, kernel_ref, gain_ref, w_in_hbm, w_out_hbm, cot_hbm, grid_hbm,
                share_ref, grad_grid, o0, o1, o2, o3, o4,
                grid, near, taps, conv, gwi, gwo, rims, normed_ref, xhat_ref, inv_ref, gn_ref,
                cot_ref, w_in_ref, w_out_ref, acc, sems, *, slots):
    own = own_ref[0]
    copies = [
        pltpu.make_async_copy(src, dst, sems.at[k])
        for k, (src, dst) in enumerate(
            ((grid_hbm, grid), (w_in_hbm, w_in_ref), (w_out_hbm, w_out_ref), (cot_hbm, cot_ref))
        )
    ]
    for copy in copies:
        copy.start()
    fetch_strips(near_ids, own, slots, (s0, s1, s2, s3, s4), near)
    spread_taps(kernel_ref, taps)
    copies[0].wait()
    put_halo(near, grid)
    grid3 = grid.reshape(TALL * WIDE, 8, 128)
    convolve(grid3, taps, False, conv.reshape(HALF * SIZE, 8, 128))
    gain = gain_ref[...]
    lines = ROWS // SIZE

    def where(n):
        return (n % 2) * lines, place((n // 2) % 2, n // 4, 0)

    def normalise(n, carry):
        first, spot = where(n)
        cells = pl.ds(pl.multiple_of(n * ROWS, ROWS), ROWS)
        cv = jnp.concatenate(
            [
                jnp.concatenate(
                    [conv[pl.ds((first + r) * SIZE * 8 + spot + part, SIZE, stride=8), :] for part in range(2)], axis=1
                )
                for r in range(lines)
            ],
            axis=0,
        )
        cv = cv - jnp.mean(cv, axis=-1, keepdims=True)
        inv = lax.rsqrt(jnp.mean(cv * cv, axis=-1, keepdims=True) + 1e-06)
        xhat = cv * inv
        xhat_ref[cells, :] = xhat
        inv_ref[cells, :] = jnp.broadcast_to(inv, (ROWS, 128))
        normed_ref[cells, :] = (xhat * gain).astype(BF16)
        return carry

    lax.fori_loop(0, 2 * SIZE * SIZE // ROWS, normalise, 0)
    for copy in copies[1:]:
        copy.wait()
    steps = [(t, slice(f * 256, f * 256 + 256)) for t in range(2) for f in range(FF // 256)]
    cells_of = [slice(t * SIZE * SIZE, (t + 1) * SIZE * SIZE) for t in range(2)]
    across = (((1,), (1,)), ((), ()))

    def forward(step):
        t, cols = step
        pre = jnp.dot(normed_ref[cells_of[t], :], w_in_ref[:, cols], preferred_element_type=F32)
        return pre, lax.dot_general(cot_ref[cells_of[t], :], w_out_ref[cols, :], across, preferred_element_type=F32)

    ahead = forward(steps[0])
    for k, (t, cols) in enumerate(steps):
        pre, gact = ahead
        if k + 1 < len(steps):
            ahead = forward(steps[k + 1])
        if cols.start == 0:
            normed_t = normed_ref[cells_of[t], :].T
            cot_t = cot_ref[cells_of[t], :].T
        act, slope = gelu_parts(pre)
        act = act.astype(BF16)
        gpre = (gact * slope).astype(BF16)
        one = jnp.dot(normed_t, gpre, preferred_element_type=F32)
        two = jnp.dot(cot_t, act, preferred_element_type=F32)
        gn = lax.dot_general(gpre, w_in_ref[:, cols], across, preferred_element_type=F32)
        if t == 0:
            gwi[:, cols] = one
            gwo[:, cols] = two
        else:
            gwi[:, cols] += one
            gwo[:, cols] += two
        if cols.start == 0:
            gn_ref[cells_of[t], :] = gn
        else:
            gn_ref[cells_of[t], :] += gn

    def denormalise(n, ggain):
        first, spot = where(n)
        cells = pl.ds(pl.multiple_of(n * ROWS, ROWS), ROWS)
        gn, xhat = gn_ref[cells, :], xhat_ref[cells, :]
        inv = inv_ref[cells, 0:1]
        ggain = ggain + jnp.sum((gn * xhat).reshape(ROWS // 8, 8, CH), axis=0)
        gx = gn * gain
        m1 = jnp.mean(gx, axis=-1, keepdims=True)
        m2 = jnp.mean(gx * xhat, axis=-1, keepdims=True)
        gc = (inv * (gx - m1 - xhat * m2)).astype(BF16).astype(F32)
        for r in range(lines):
            piece = gc[r * SIZE : (r + 1) * SIZE]
            at = ((first + r + RIM) * WIDE + RIM) * 8 + spot
            for part in range(2):
                grad_grid[pl.ds(at + part, SIZE, stride=8), :] = piece[:, lanes_of(part)]
        return ggain

    ggain = lax.fori_loop(0, 2 * SIZE * SIZE // ROWS, denormalise, jnp.zeros((8, CH), F32))
    low = lax.broadcasted_iota(jnp.int32, (CH, 128), 1) < 64
    for p in range(FF // 128):
        one = gwi[:, p * 128 : p * 128 + 128]
        two = gwo[:, p * 128 : p * 128 + 128]
        even = jnp.where(low, one, pltpu.roll(two, 64, 1)).astype(BF16)
        odd = jnp.where(low, pltpu.roll(one, 64, 1), two).astype(BF16)
        for k in range(NEAR_GROUP):
            share_ref[2 * p, PIECE * k : PIECE * k + 32] = even[32 * k : 32 * k + 32]
            share_ref[2 * p + 1, PIECE * k : PIECE * k + 32] = odd[32 * k : 32 * k + 32]
    tap_gradients(grid3, grad_grid.reshape(TALL * WIDE, 8, 128), ggain, acc, share_ref)
    for t in range(2):
        for part in range(2):
            for r in range(RIM):
                for half, at, other in ((0, RIM + HALF + r, RIM + r), (1, r, HALF + r)):
                    mine = ((at * WIDE) + RIM) * 8 + place(half, t, part)
                    theirs = ((other * WIDE) + RIM) * 8 + place(1 - half, t, part)
                    grad_grid[pl.ds(mine, SIZE, stride=8), :] = grad_grid[pl.ds(theirs, SIZE, stride=8), :]
            lanes = lanes_of(part)
            for k in range(RIM):
                top = ((RIM + k) * WIDE + RIM) * 8 + place(0, t, part)
                bottom = ((HALF + k) * WIDE + RIM) * 8 + place(1, t, part)
                rims[4 * t, k, :, lanes] = grad_grid[pl.ds(top, SIZE, stride=8), :].astype(BF16)
                rims[4 * t + 1, k, :, lanes] = grad_grid[pl.ds(bottom, SIZE, stride=8), :].astype(BF16)
                for side, col in ((2, RIM + k), (3, SIZE + k)):
                    both = [
                        grad_grid[pl.ds((RIM * WIDE + col) * 8 + place(half, t, part), HALF, stride=WIDE * 8), :]
                        for half in range(2)
                    ]
                    rims[4 * t + side, k, :, lanes] = jnp.concatenate(both, axis=0).astype(BF16)
    send_strips(near_ids, own, slots, rims, (o0, o1, o2, o3, o4))


def tap_gradients(grid3, grad3, ggain, acc, share_ref):
    acc[...] = jnp.zeros_like(acc)

    def column(j, carry):
        g = [grad3[(RIM + r) * WIDE + RIM + j] for r in range(HALF)]
        for q in range(TAPS):
            terms = [grid3[(r + q // KW) * WIDE + j + q % KW] * g[r] for r in range(HALF)]
            while len(terms) > 1:
                terms = [terms[k] + terms[k + 1] for k in range(0, len(terms), 2)]
            acc[q] += terms[0]
        return carry

    lax.fori_loop(0, SIZE, column, 0)
    even = lax.rem(lax.broadcasted_iota(jnp.int32, (8, 128), 0), 2) == 0
    sums = [[], []]
    for q in range(TAPS):
        one = acc[q]
        sums[0].append(jnp.sum(jnp.where(even, one, 0.0), axis=0, keepdims=True))
        sums[1].append(jnp.sum(jnp.where(even, 0.0, one), axis=0, keepdims=True))
    for part in range(2):
        sums[part].append(jnp.sum(ggain[:, lanes_of(part)], axis=0, keepdims=True))
        sums[part].append(jnp.zeros((PART_ROWS - TAPS - 1, 128), F32))
    total = jnp.concatenate(sums[0] + sums[1], axis=0).astype(BF16)
    for d in range(16):
        for k in range(NEAR_GROUP):
            share_ref[d, PIECE * k + 32 : PIECE * k + 48] = total[16 * k : 16 * k + 16]


def back_kernel(own_ref, near_ids, s0, s1, s2, s3, s4, kernel_ref, cot_ref, grid_hbm, out_ref, grid, near, taps, conv, sem, *, slots):
    copy = pltpu.make_async_copy(grid_hbm, grid, sem)
    copy.start()
    fetch_strips(near_ids, own_ref[0], slots, (s0, s1, s2, s3, s4), near)
    spread_taps(kernel_ref, taps)
    copy.wait()
    put_halo(near, grid)
    convolve(grid.reshape(TALL * WIDE, 8, 128), taps, True, conv.reshape(HALF * SIZE, 8, 128))
    for t in range(2):
        for i in range(SIZE):
            out_ref[t, i] = (cot_ref[t, i].astype(F32) + rows_of(conv, t, i // HALF, i % HALF)).astype(BF16)


def last_kernel(in_ref, w_in_ref, w_out_ref, taps_ref, gain_ref, low, *, scale):
    weights = (in_ref[:, 0:32, :].astype(F32) * scale).reshape(CH, 128).T
    w_in_ref[...] = weights[0:64, :]
    w_out_ref[...] = weights[64:128, :]
    low[...] = (in_ref[:, 32:48, :].astype(F32) * scale).reshape(2 * PART_ROWS, 128)
    for part in range(2):
        lanes = lanes_of(part)
        for a in range(KW):
            at = part * PART_ROWS + a * KW
            taps_ref[a, :, lanes] = low[at : at + KW, :]
        at = part * PART_ROWS + TAPS
        gain_ref[:, lanes] = low[at : at + 1, :]


SMEM = pl.BlockSpec(memory_space=pltpu.SMEM)
STRIPS = tuple(jax.ShapeDtypeStruct((n, RIM, SIZE, CH), BF16) for n in COUNTS)
RIMS = pltpu.VMEM((8, RIM, SIZE, CH), BF16)
NEAR = pltpu.VMEM((16, RIM, SIZE, CH), F32)
GRID = jax.ShapeDtypeStruct((TALL * WIDE * 8, 128), F32)
GRID_SPACE = pltpu.VMEM(GRID.shape, F32)
SPREAD = pltpu.VMEM((TAPS, 8, 128), F32)
CONV = pltpu.VMEM((HALF * SIZE * 8, 128), F32)


def call(kernel, name, out, scalars, arrays, scratch=(), far=(), flops=10**6, moved=10**6, vmem_mib=24):
    vmem = pl.BlockSpec(memory_space=pltpu.VMEM)
    anywhere = pl.BlockSpec(memory_space=pl.ANY)
    return pl.pallas_call(
        kernel,
        out_shape=out,
        in_specs=[SMEM] * len(scalars) + [vmem] * len(arrays) + [anywhere] * len(far),
        out_specs=[vmem] * len(out) if isinstance(out, tuple) else vmem,
        scratch_shapes=scratch,
        compiler_params=pltpu.CompilerParams(vmem_limit_bytes=vmem_mib * 1024 * 1024),
        cost_estimate=pl.CostEstimate(flops=flops, bytes_accessed=moved, transcendentals=0),
        name=name,
    )(*scalars, *arrays, *far)


def exchange(strips):
    n = lax.axis_size("tiles")
    got = {0: strips[0]}
    for off, strip in zip(OFFSETS[1:], strips[1:]):
        got[-off] = lax.ppermute(strip, "tiles", [(i, (i + off) % n) for i in range(n)])
    return tuple(got[off] for off in OFFSETS)


def sum_of(pieces):
    return jnp.sum(pieces.astype(F32), axis=0)


def copies_of(piece, count):
    return jnp.broadcast_to(piece[None], (count, *piece.shape))


def group_exchange(pieces, groups):
    return lax.all_to_all(pieces, "tiles", 0, 0, tiled=True, axis_index_groups=groups)


def body(fields, neighbours, kernel, gain, w_in, w_out, cotangent):
    n_tiles, n_dp = lax.axis_size("tiles"), lax.axis_size("dp")
    slots = 2 * n_tiles
    scalars = (lax.axis_index("tiles").reshape(1).astype(jnp.int32), neighbours)
    tiles, cot = fields[0], cotangent[0]
    stage = pltpu.VMEM((2, SIZE * 16, 128), F32)
    sent = call(functools.partial(rim_kernel, slots=slots), "rims", STRIPS, scalars, (tiles,), (RIMS, stage))
    grid = call(grid_kernel, "grid", GRID, (), (tiles,), moved=5 * 10**6)
    got = exchange(sent)
    cells = 2 * SIZE * SIZE
    share, grad_grid, *sent = call(
        functools.partial(main_kernel, slots=slots),
        "main",
        (jax.ShapeDtypeStruct((16, NEAR_GROUP * PIECE, 128), BF16), GRID, *STRIPS),
        scalars,
        (*got, kernel, gain.reshape(1, CH)),
        (
            GRID_SPACE, NEAR, SPREAD, CONV, pltpu.VMEM((CH, FF), F32), pltpu.VMEM((CH, FF), F32), RIMS,
            pltpu.VMEM((cells, CH), BF16), pltpu.VMEM((cells, CH), F32), pltpu.VMEM((cells, 128), F32),
            pltpu.VMEM((cells, CH), F32), pltpu.VMEM((cells, CH), BF16), pltpu.VMEM((CH, FF), BF16),
            pltpu.VMEM((FF, CH), BF16), pltpu.VMEM((TAPS, 8, 128), F32), pltpu.SemaphoreType.DMA((4,)),
        ),
        far=(w_in, w_out, cot.reshape(cells, CH), grid),
        flops=40 * 10**9,
        vmem_mib=48,
    )
    share = lax.all_to_all(share, "dp", 0, 0, tiled=True)
    share, got = lax.optimization_barrier((share, exchange(sent)))
    grad_fields = call(
        functools.partial(back_kernel, slots=slots),
        "back",
        jax.ShapeDtypeStruct((2, SIZE, SIZE, CH), BF16),
        scalars,
        (*got, kernel, cot),
        (GRID_SPACE, NEAR, SPREAD, CONV, pltpu.SemaphoreType.DMA(())),
        far=(grad_grid,),
        flops=12 * 10**9,
    )
    cut = sum_of(share)
    near = [list(range(g, g + NEAR_GROUP)) for g in range(0, n_tiles, NEAR_GROUP)]
    far = [list(range(g, n_tiles, NEAR_GROUP)) for g in range(NEAR_GROUP)]
    cut = group_exchange(cut.astype(BF16).reshape(NEAR_GROUP, PIECE, 128), near)
    cut = group_exchange(copies_of(sum_of(cut), len(far[0])), far)
    cut, grad_fields = lax.optimization_barrier((cut, grad_fields))
    cut = group_exchange(copies_of(sum_of(cut).astype(BF16), NEAR_GROUP), near)
    scale = float((n_dp * slots * SIZE * SIZE) ** -0.5)
    g_in, g_out, g_taps, g_gain = call(
        functools.partial(last_kernel, scale=scale),
        "last",
        (
            jax.ShapeDtypeStruct((64, CH), F32),
            jax.ShapeDtypeStruct((64, CH), F32),
            jax.ShapeDtypeStruct((KW, KW, CH), F32),
            jax.ShapeDtypeStruct((1, CH), F32),
        ),
        (),
        (cut,),
        (pltpu.VMEM((2 * PART_ROWS, 128), F32),),
    )
    return grad_fields[None], g_in.T, g_out, g_taps, g_gain.reshape(CH)


def solution(mesh):
    return jax.shard_map(
        body,
        mesh=mesh,
        in_specs=(
            P("dp", "tiles", None, None, None),
            P("tiles", None),
            P(),
            P(),
            P(),
            P(),
            P("dp", "tiles", None, None, None),
        ),
        out_specs=(P("dp", "tiles", None, None, None), P(None, "dp"), P("dp", None), P(), P()),
        check_vma=False,
    )
```

```python
import functools

import jax
import jax.numpy as jnp
from jax import lax
from jax.experimental import pallas as pl
from jax.experimental.pallas import tpu as pltpu
from jax.sharding import PartitionSpec as P

KW = 7
TAPS = KW * KW
RIM = KW // 2
SIZE = 32
WIDE = SIZE + 2 * RIM
HALF = SIZE // 2
TALL = HALF + 2 * RIM
CH = 256
FF = 1024
NEAR_GROUP = 8
PIECE = 48
PART_ROWS = 64
ROWS = 256
F32 = jnp.float32
BF16 = jnp.bfloat16
OFFSETS = (0, -1, 1, -2, 2)
PAIRS = (
    ((0, 1), (1, 0)),
    ((0, 0), (0, 1), (1, 0), (1, 1)),
    ((0, 0), (0, 1), (1, 0), (1, 1)),
    ((0, 0), (0, 1), (1, 1)),
    ((0, 0), (1, 0), (1, 1)),
)
COUNTS = tuple(len(p) for p in PAIRS)
RIM_OF = (0, 1, 2, 3, 0, 0, 1, 1)


def place(half, tile, part):
    return 4 * half + 2 * tile + part


def lanes_of(part):
    return slice(part * 128, part * 128 + 128)


def put_row(grid, pitch, tile, row, first, value):
    count = value.shape[0]
    for half in range(2):
        i = row - HALF * half
        if 0 <= i < TALL:
            for part in range(2):
                at = (i * pitch + first) * 8 + place(half, tile, part)
                grid[pl.ds(at, count, stride=8), :] = value[:, lanes_of(part)]


def put_column(grid, tile, col, value):
    for half in range(2):
        lo = max(0, HALF * half - RIM)
        hi = min(SIZE, HALF * half + HALF + RIM)
        for part in range(2):
            at = ((lo + RIM - HALF * half) * WIDE + col) * 8 + place(half, tile, part)
            grid[pl.ds(at, hi - lo, stride=WIDE * 8), :] = value[lo:hi, lanes_of(part)]


def fetch_strips(near_ids, own, slots, strips, near):
    def fetch(p, carry):
        t, d = p // 8, p % 8
        slot = near_ids[t, d]
        other = slot // 2
        s = slot - 2 * other
        off = lax.rem(other - own + slots // 2 + slots // 4, slots // 2) - slots // 4
        off = jnp.where(slot < 0, slots, off)

        @pl.when(slot < 0)
        def _():
            near[p] = jnp.zeros((RIM, SIZE, CH), F32)

        for strip, offset in zip(strips, OFFSETS):
            index = s if offset == 0 else 2 * s + t if abs(offset) == 1 else s + t

            @pl.when(off == offset)
            def _(strip=strip, index=index):
                near[p] = strip[index].astype(F32)

        return carry

    lax.fori_loop(0, 16, fetch, 0)


def load(sources, targets, sems):
    copies = [pltpu.make_async_copy(src, dst, sems.at[k]) for k, (src, dst) in enumerate(zip(sources, targets))]
    for copy in copies:
        copy.start()
    return copies


def wait_all(copies):
    for copy in copies:
        copy.wait()


def put_tiles(tile_ref, grid):
    for t in range(2):
        for i in range(SIZE):
            put_row(grid, WIDE, t, RIM + i, RIM, tile_ref[t, i].astype(F32))


def put_halo(near, grid):
    for t in range(2):
        for i in range(RIM):
            for row, mid, west, east in ((i, 0, 4, 5), (RIM + SIZE + i, 1, 6, 7)):
                put_row(grid, WIDE, t, row, 0, near[t * 8 + west, i, SIZE - RIM : SIZE, :])
                put_row(grid, WIDE, t, row, RIM, near[t * 8 + mid, i])
                put_row(grid, WIDE, t, row, RIM + SIZE, near[t * 8 + east, i, 0:RIM, :])
        for k in range(RIM):
            put_column(grid, t, k, near[t * 8 + 2, k])
            put_column(grid, t, RIM + SIZE + k, near[t * 8 + 3, k])


def pick_rim(near_ids, own, slots, s, offset, t):
    slot = lax.rem(2 * own + 2 * offset + t + slots, slots)
    rim = jnp.int32(0)
    for d in range(8):
        rim = jnp.where(near_ids[s, d] == slot, RIM_OF[d], rim)
    return 4 * s + rim


def send_strips(near_ids, own, slots, rims, outs):
    for out, offset, pairs in zip(outs, OFFSETS, PAIRS):
        for k, (s, t) in enumerate(pairs):
            out[k] = rims[pick_rim(near_ids, own, slots, s, offset, t)]


def spread_taps(kernel_ref, taps):
    even = lax.rem(lax.broadcasted_iota(jnp.int32, (8, 128), 0), 2) == 0
    for a in range(KW):
        for b in range(KW):
            low = jnp.broadcast_to(kernel_ref[a, b : b + 1, 0:128], (8, 128))
            high = jnp.broadcast_to(kernel_ref[a, b : b + 1, 128:256], (8, 128))
            taps[a * KW + b] = jnp.where(even, low, high)


def convolve(grid3, taps, flip, out3):
    def column(j, carry):
        acc = [None] * HALF
        for q in range(TAPS):
            tap = taps[TAPS - 1 - q if flip else q]
            for r in range(HALF):
                term = grid3[(r + q // KW) * WIDE + j + q % KW] * tap
                acc[r] = term if acc[r] is None else acc[r] + term
        for r in range(HALF):
            out3[r * SIZE + j] = acc[r]
        return carry

    lax.fori_loop(0, SIZE, column, 0)


def rows_of(flat, tile, half, r):
    return jnp.concatenate(
        [flat[pl.ds(r * SIZE * 8 + place(half, tile, part), SIZE, stride=8), :] for part in range(2)], axis=1
    )


def gelu_parts(x):
    size = jnp.abs(x)
    t = pl.reciprocal(1.0 + (0.3275911 * 0.7071067811865476) * size, approx=False)
    bell = jnp.exp2((-0.5 * 1.4426950408889634) * (x * x))
    poly = 0.5 * 1.061405429 * t - 0.5 * 1.453152027
    poly = poly * t + 0.5 * 1.421413741
    poly = poly * t - 0.5 * 0.284496736
    poly = poly * t + 0.5 * 0.254829592
    tail = poly * t * bell
    cdf = jnp.where(x < 0, tail, 1.0 - tail)
    return x * cdf, cdf + x * (bell * 0.3989422804014327)


def rim_kernel(own_ref, near_hbm, tile_hbm, *rest, slots):
    outs, (near_ids, tile_ref, rims, stage, sems) = rest[:5], rest[5:]
    wait_all(load((near_hbm, tile_hbm), (near_ids, tile_ref), sems))
    for s in range(2):
        rims[4 * s] = tile_ref[s, 0:RIM]
        rims[4 * s + 1] = tile_ref[s, SIZE - RIM : SIZE]
        for side, first, row in ((2, 0, 0), (3, 16, 16 - RIM)):
            for part in range(2):
                stage[part] = tile_ref[s, :, first : first + 16, lanes_of(part)].astype(F32).reshape(SIZE * 16, 128)
                for k in range(RIM):
                    rims[4 * s + side, k, :, lanes_of(part)] = stage[part, pl.ds(row + k, SIZE, stride=16), :].astype(BF16)
    send_strips(near_ids, own_ref[0], slots, rims, outs)


def main_kernel(own_ref, near_hbm, h0, h1, h2, h3, h4, tile_hbm, kernel_hbm, gain_hbm, w_in_hbm, w_out_hbm, cot_hbm,
                share_hbm, grad_hbm, o0, o1, o2, o3, o4,
                near_ids, s0, s1, s2, s3, s4, tile_ref, kernel_ref, gain_ref, w_in_ref, w_out_ref, cot_ref,
                grid, near, taps, conv, gwi, gwo, rims, normed_ref, xhat_ref, inv_ref, gn_ref,
                acc, share_ref, grad_grid, grad_ref, sems, out_sems, *, slots):
    own = own_ref[0]
    copies = load(
        (tile_hbm, near_hbm, h0, h1, h2, h3, h4, kernel_hbm, gain_hbm, w_in_hbm, w_out_hbm, cot_hbm),
        (tile_ref, near_ids, s0, s1, s2, s3, s4, kernel_ref, gain_ref, w_in_ref, w_out_ref, cot_ref),
        sems,
    )
    copies[0].wait()
    put_tiles(tile_ref, grid)
    wait_all(copies[1:9])
    fetch_strips(near_ids, own, slots, (s0, s1, s2, s3, s4), near)
    spread_taps(kernel_ref, taps)
    put_halo(near, grid)
    grid3 = grid.reshape(TALL * WIDE, 8, 128)
    convolve(grid3, taps, False, conv.reshape(HALF * SIZE, 8, 128))
    gain = gain_ref[...]
    lines = ROWS // SIZE

    def where(n):
        return (n % 2) * lines, place((n // 2) % 2, n // 4, 0)

    def normalise(n, carry):
        first, spot = where(n)
        cells = pl.ds(pl.multiple_of(n * ROWS, ROWS), ROWS)
        cv = jnp.concatenate(
            [
                jnp.concatenate(
                    [conv[pl.ds((first + r) * SIZE * 8 + spot + part, SIZE, stride=8), :] for part in range(2)], axis=1
                )
                for r in range(lines)
            ],
            axis=0,
        )
        cv = cv - jnp.mean(cv, axis=-1, keepdims=True)
        inv = lax.rsqrt(jnp.mean(cv * cv, axis=-1, keepdims=True) + 1e-06)
        xhat = cv * inv
        xhat_ref[cells, :] = xhat
        inv_ref[cells, :] = jnp.broadcast_to(inv, (ROWS, 128))
        normed_ref[cells, :] = (xhat * gain).astype(BF16)
        return carry

    lax.fori_loop(0, 2 * SIZE * SIZE // ROWS, normalise, 0)
    wait_all(copies[9:])
    steps = [(t, slice(f * 256, f * 256 + 256)) for t in range(2) for f in range(FF // 256)]
    cells_of = [slice(t * SIZE * SIZE, (t + 1) * SIZE * SIZE) for t in range(2)]
    across = (((1,), (1,)), ((), ()))

    def forward(step):
        t, cols = step
        pre = jnp.dot(normed_ref[cells_of[t], :], w_in_ref[:, cols], preferred_element_type=F32)
        return pre, lax.dot_general(cot_ref[cells_of[t], :], w_out_ref[cols, :], across, preferred_element_type=F32)

    ahead = forward(steps[0])
    for k, (t, cols) in enumerate(steps):
        pre, gact = ahead
        if k + 1 < len(steps):
            ahead = forward(steps[k + 1])
        if cols.start == 0:
            normed_t = normed_ref[cells_of[t], :].T
            cot_t = cot_ref[cells_of[t], :].T
        act, slope = gelu_parts(pre)
        act = act.astype(BF16)
        gpre = (gact * slope).astype(BF16)
        one = jnp.dot(normed_t, gpre, preferred_element_type=F32)
        two = jnp.dot(cot_t, act, preferred_element_type=F32)
        gn = lax.dot_general(gpre, w_in_ref[:, cols], across, preferred_element_type=F32)
        if t == 0:
            gwi[:, cols] = one
            gwo[:, cols] = two
        else:
            gwi[:, cols] += one
            gwo[:, cols] += two
        if cols.start == 0:
            gn_ref[cells_of[t], :] = gn
        else:
            gn_ref[cells_of[t], :] += gn

    def denormalise(n, ggain):
        first, spot = where(n)
        cells = pl.ds(pl.multiple_of(n * ROWS, ROWS), ROWS)
        gn, xhat = gn_ref[cells, :], xhat_ref[cells, :]
        inv = inv_ref[cells, 0:1]
        ggain = ggain + jnp.sum((gn * xhat).reshape(ROWS // 8, 8, CH), axis=0)
        gx = gn * gain
        m1 = jnp.mean(gx, axis=-1, keepdims=True)
        m2 = jnp.mean(gx * xhat, axis=-1, keepdims=True)
        gc = (inv * (gx - m1 - xhat * m2)).astype(BF16)
        grad_ref[cells, :] = gc
        gc = gc.astype(F32)
        for r in range(lines):
            piece = gc[r * SIZE : (r + 1) * SIZE]
            at = ((first + r + RIM) * WIDE + RIM) * 8 + spot
            for part in range(2):
                grad_grid[pl.ds(at + part, SIZE, stride=8), :] = piece[:, lanes_of(part)]
        return ggain

    ggain = lax.fori_loop(0, 2 * SIZE * SIZE // ROWS, denormalise, jnp.zeros((8, CH), F32))
    results = [pltpu.make_async_copy(grad_ref, grad_hbm, out_sems.at[0])]
    results[0].start()

    def send_rows(first, count, sem):
        for k in range(NEAR_GROUP):
            rows = pl.ds(PIECE * k + first, count)
            results.append(pltpu.make_async_copy(share_ref.at[:, rows], share_hbm.at[:, rows], out_sems.at[sem + k]))
            results[-1].start()

    low = lax.broadcasted_iota(jnp.int32, (CH, 128), 1) < 64
    for p in range(FF // 128):
        one = gwi[:, p * 128 : p * 128 + 128]
        two = gwo[:, p * 128 : p * 128 + 128]
        even = jnp.where(low, one, pltpu.roll(two, 64, 1)).astype(BF16)
        odd = jnp.where(low, pltpu.roll(one, 64, 1), two).astype(BF16)
        for k in range(NEAR_GROUP):
            share_ref[2 * p, PIECE * k : PIECE * k + 32] = even[32 * k : 32 * k + 32]
            share_ref[2 * p + 1, PIECE * k : PIECE * k + 32] = odd[32 * k : 32 * k + 32]
    send_rows(0, 32, 1)
    tap_gradients(grid3, grad_grid.reshape(TALL * WIDE, 8, 128), ggain, acc, share_ref)
    send_rows(32, 16, 1 + NEAR_GROUP)
    for t in range(2):
        for part in range(2):
            lanes = lanes_of(part)
            for k in range(RIM):
                top = ((RIM + k) * WIDE + RIM) * 8 + place(0, t, part)
                bottom = ((HALF + k) * WIDE + RIM) * 8 + place(1, t, part)
                rims[4 * t, k, :, lanes] = grad_grid[pl.ds(top, SIZE, stride=8), :].astype(BF16)
                rims[4 * t + 1, k, :, lanes] = grad_grid[pl.ds(bottom, SIZE, stride=8), :].astype(BF16)
                for side, col in ((2, RIM + k), (3, SIZE + k)):
                    both = [
                        grad_grid[pl.ds((RIM * WIDE + col) * 8 + place(half, t, part), HALF, stride=WIDE * 8), :]
                        for half in range(2)
                    ]
                    rims[4 * t + side, k, :, lanes] = jnp.concatenate(both, axis=0).astype(BF16)
    send_strips(near_ids, own, slots, rims, (o0, o1, o2, o3, o4))
    wait_all(results)


def tap_gradients(grid3, grad3, ggain, acc, share_ref):
    acc[...] = jnp.zeros_like(acc)

    def column(j, carry):
        g = [grad3[(RIM + r) * WIDE + RIM + j] for r in range(HALF)]
        for q in range(TAPS):
            terms = [grid3[(r + q // KW) * WIDE + j + q % KW] * g[r] for r in range(HALF)]
            while len(terms) > 1:
                terms = [terms[k] + terms[k + 1] for k in range(0, len(terms), 2)]
            acc[q] += terms[0]
        return carry

    lax.fori_loop(0, SIZE, column, 0)
    even = lax.rem(lax.broadcasted_iota(jnp.int32, (8, 128), 0), 2) == 0
    sums = [[], []]
    for q in range(TAPS):
        one = acc[q]
        sums[0].append(jnp.sum(jnp.where(even, one, 0.0), axis=0, keepdims=True))
        sums[1].append(jnp.sum(jnp.where(even, 0.0, one), axis=0, keepdims=True))
    for part in range(2):
        sums[part].append(jnp.sum(ggain[:, lanes_of(part)], axis=0, keepdims=True))
        sums[part].append(jnp.zeros((PART_ROWS - TAPS - 1, 128), F32))
    total = jnp.concatenate(sums[0] + sums[1], axis=0).astype(BF16)
    for d in range(16):
        for k in range(NEAR_GROUP):
            share_ref[d, PIECE * k + 32 : PIECE * k + 48] = total[16 * k : 16 * k + 16]


def back_kernel(own_ref, near_hbm, h0, h1, h2, h3, h4, grad_hbm, kernel_hbm, cot_hbm, out_ref,
                near_ids, s0, s1, s2, s3, s4, grad_ref, kernel_ref, cot_ref, grid, near, taps, conv, sems, *, slots):
    copies = load(
        (grad_hbm, near_hbm, h0, h1, h2, h3, h4, kernel_hbm, cot_hbm),
        (grad_ref, near_ids, s0, s1, s2, s3, s4, kernel_ref, cot_ref),
        sems,
    )
    copies[0].wait()
    put_tiles(grad_ref, grid)
    wait_all(copies[1:])
    fetch_strips(near_ids, own_ref[0], slots, (s0, s1, s2, s3, s4), near)
    spread_taps(kernel_ref, taps)
    put_halo(near, grid)
    convolve(grid.reshape(TALL * WIDE, 8, 128), taps, True, conv.reshape(HALF * SIZE, 8, 128))
    for t in range(2):
        for i in range(SIZE):
            out_ref[t, i] = (cot_ref[t, i].astype(F32) + rows_of(conv, t, i // HALF, i % HALF)).astype(BF16)


def sum_kernel(in_ref, out_ref):
    out_ref[...] = jnp.sum(in_ref[...].astype(F32), axis=0).astype(BF16)


def last_kernel(in_ref, w_in_ref, w_out_ref, taps_ref, gain_ref, low, *, scale):
    weights = (in_ref[:, 0:32, :].astype(F32) * scale).reshape(CH, 128).T
    w_in_ref[...] = weights[0:64, :]
    w_out_ref[...] = weights[64:128, :]
    low[...] = (in_ref[:, 32:48, :].astype(F32) * scale).reshape(2 * PART_ROWS, 128)
    for part in range(2):
        lanes = lanes_of(part)
        for a in range(KW):
            at = part * PART_ROWS + a * KW
            taps_ref[a, :, lanes] = low[at : at + KW, :]
        at = part * PART_ROWS + TAPS
        gain_ref[:, lanes] = low[at : at + 1, :]


SMEM = pl.BlockSpec(memory_space=pltpu.SMEM)
STRIPS = tuple(jax.ShapeDtypeStruct((n, RIM, SIZE, CH), BF16) for n in COUNTS)
RIMS = pltpu.VMEM((8, RIM, SIZE, CH), BF16)
NEAR = pltpu.VMEM((16, RIM, SIZE, CH), F32)
GRID = jax.ShapeDtypeStruct((TALL * WIDE * 8, 128), F32)
GRID_SPACE = pltpu.VMEM(GRID.shape, F32)
SPREAD = pltpu.VMEM((TAPS, 8, 128), F32)
CELLS = 2 * SIZE * SIZE
SHARE = jax.ShapeDtypeStruct((16, NEAR_GROUP * PIECE, 128), BF16)
CONV = pltpu.VMEM((HALF * SIZE * 8, 128), F32)


IDS = pltpu.SMEM((2, 8), jnp.int32)
TILES = pltpu.VMEM((2, SIZE, SIZE, CH), BF16)
LANDED = (IDS, *(pltpu.VMEM(x.shape, BF16) for x in STRIPS), TILES, pltpu.VMEM((KW, KW, CH), F32))
MAIN_SCRATCH = (
    *LANDED,
    pltpu.VMEM((1, CH), F32),
    pltpu.VMEM((CH, FF), BF16),
    pltpu.VMEM((FF, CH), BF16),
    pltpu.VMEM((CELLS, CH), BF16),
    GRID_SPACE,
    NEAR,
    SPREAD,
    CONV,
    pltpu.VMEM((CH, FF), F32),
    pltpu.VMEM((CH, FF), F32),
    RIMS,
    pltpu.VMEM((CELLS, CH), BF16),
    pltpu.VMEM((CELLS, CH), F32),
    pltpu.VMEM((CELLS, 128), F32),
    pltpu.VMEM((CELLS, CH), F32),
    SPREAD,
    pltpu.VMEM(SHARE.shape, BF16),
    GRID_SPACE,
    pltpu.VMEM((CELLS, CH), BF16),
    pltpu.SemaphoreType.DMA((12,)),
    pltpu.SemaphoreType.DMA((1 + 2 * NEAR_GROUP,)),
)


def call(kernel, name, out, scalars, arrays, scratch=(), far=(), far_outs=0, flops=10**6, moved=10**6, vmem_mib=24):
    vmem = pl.BlockSpec(memory_space=pltpu.VMEM)
    hbm = pl.BlockSpec(memory_space=pltpu.HBM)
    return pl.pallas_call(
        kernel,
        out_shape=out,
        in_specs=[SMEM] * len(scalars) + [vmem] * len(arrays) + [hbm] * len(far),
        out_specs=[hbm] * far_outs + [vmem] * (len(out) - far_outs) if isinstance(out, tuple) else vmem,
        scratch_shapes=scratch,
        compiler_params=pltpu.CompilerParams(vmem_limit_bytes=vmem_mib * 1024 * 1024),
        cost_estimate=pl.CostEstimate(flops=flops, bytes_accessed=moved, transcendentals=0),
        name=name,
    )(*scalars, *arrays, *far)


def exchange(strips):
    n = lax.axis_size("tiles")
    got = {0: strips[0]}
    for off, strip in zip(OFFSETS[1:], strips[1:]):
        got[-off] = lax.ppermute(strip, "tiles", [(i, (i + off) % n) for i in range(n)])
    return tuple(got[off] for off in OFFSETS)


def sum_of(pieces):
    return jnp.sum(pieces.astype(F32), axis=0)


def copies_of(piece, count):
    return jnp.broadcast_to(piece[None], (count, *piece.shape))


def group_exchange(pieces, groups):
    return lax.all_to_all(pieces, "tiles", 0, 0, tiled=True, axis_index_groups=groups)


def body(fields, neighbours, kernel, gain, w_in, w_out, cotangent):
    n_tiles, n_dp = lax.axis_size("tiles"), lax.axis_size("dp")
    slots = 2 * n_tiles
    own = (lax.axis_index("tiles").reshape(1).astype(jnp.int32),)
    tiles, cot = fields[0], cotangent[0]
    stage = pltpu.VMEM((2, SIZE * 16, 128), F32)
    sent = call(
        functools.partial(rim_kernel, slots=slots),
        "rims",
        STRIPS,
        own,
        (),
        (IDS, TILES, RIMS, stage, pltpu.SemaphoreType.DMA((2,))),
        far=(neighbours, tiles),
        vmem_mib=60,
    )
    got = exchange(sent)
    share, grad, *sent = call(
        functools.partial(main_kernel, slots=slots),
        "main",
        (SHARE, jax.ShapeDtypeStruct((CELLS, CH), BF16), *STRIPS),
        own,
        (),
        MAIN_SCRATCH,
        far=(neighbours, *got, tiles, kernel, gain.reshape(1, CH), w_in, w_out, cot.reshape(CELLS, CH)),
        far_outs=2,
        flops=40 * 10**9,
        vmem_mib=60,
    )
    share = lax.all_to_all(share, "dp", 0, 0, tiled=True)
    share, got = lax.optimization_barrier((share, exchange(sent)))
    grad_fields = call(
        functools.partial(back_kernel, slots=slots),
        "back",
        jax.ShapeDtypeStruct((2, SIZE, SIZE, CH), BF16),
        own,
        (),
        (*LANDED, TILES, GRID_SPACE, NEAR, SPREAD, CONV, pltpu.SemaphoreType.DMA((9,))),
        far=(neighbours, *got, grad.reshape(tiles.shape), kernel, cot),
        flops=12 * 10**9,
        vmem_mib=60,
    )
    cut = call(sum_kernel, "sum_dp", jax.ShapeDtypeStruct(SHARE.shape[1:], BF16), (), (share,), vmem_mib=16)
    near = [list(range(g, g + NEAR_GROUP)) for g in range(0, n_tiles, NEAR_GROUP)]
    far = [list(range(g, n_tiles, NEAR_GROUP)) for g in range(NEAR_GROUP)]
    cut = group_exchange(cut.reshape(NEAR_GROUP, PIECE, 128), near)
    cut = group_exchange(copies_of(sum_of(cut), len(far[0])), far)
    cut, grad_fields = lax.optimization_barrier((cut, grad_fields))
    cut = group_exchange(copies_of(sum_of(cut).astype(BF16), NEAR_GROUP), near)
    scale = float((n_dp * slots * SIZE * SIZE) ** -0.5)
    g_in, g_out, g_taps, g_gain = call(
        functools.partial(last_kernel, scale=scale),
        "last",
        (
            jax.ShapeDtypeStruct((64, CH), F32),
            jax.ShapeDtypeStruct((64, CH), F32),
            jax.ShapeDtypeStruct((KW, KW, CH), F32),
            jax.ShapeDtypeStruct((1, CH), F32),
        ),
        (),
        (cut,),
        (pltpu.VMEM((2 * PART_ROWS, 128), F32),),
    )
    return grad_fields[None], g_in.T, g_out, g_taps, g_gain.reshape(CH)


def solution(mesh):
    return jax.shard_map(
        body,
        mesh=mesh,
        in_specs=(
            P("dp", "tiles", None, None, None),
            P("tiles", None),
            P(),
            P(),
            P(),
            P(),
            P("dp", "tiles", None, None, None),
        ),
        out_specs=(P("dp", "tiles", None, None, None), P(None, "dp"), P("dp", None), P(), P()),
        check_vma=False,
    )
```

```python
import functools

import jax
import jax.numpy as jnp
from jax import lax
from jax.experimental import pallas as pl
from jax.experimental.pallas import tpu as pltpu
from jax.sharding import PartitionSpec as P

KW = 7
TAPS = KW * KW
RIM = KW // 2
SIZE = 32
WIDE = SIZE + 2 * RIM
HALF = SIZE // 2
TALL = HALF + 2 * RIM
CH = 256
FF = 1024
NEAR_GROUP = 8
PIECE = 48
PART_ROWS = 64
ROWS = 512
F32 = jnp.float32
BF16 = jnp.bfloat16
OFFSETS = (0, -1, 1, -2, 2)
PAIRS = (
    ((0, 1), (1, 0)),
    ((0, 0), (0, 1), (1, 0), (1, 1)),
    ((0, 0), (0, 1), (1, 0), (1, 1)),
    ((0, 0), (0, 1), (1, 1)),
    ((0, 0), (1, 0), (1, 1)),
)
COUNTS = tuple(len(p) for p in PAIRS)
RIM_OF = (0, 1, 2, 3, 0, 0, 1, 1)


def place(half, tile, part):
    return 4 * half + 2 * tile + part


def lanes_of(part):
    return slice(part * 128, part * 128 + 128)


def put_row(grid, pitch, tile, row, first, value):
    count = value.shape[0]
    for half in range(2):
        i = row - HALF * half
        if 0 <= i < TALL:
            for part in range(2):
                at = (i * pitch + first) * 8 + place(half, tile, part)
                grid[pl.ds(at, count, stride=8), :] = value[:, lanes_of(part)]


def put_column(grid, tile, col, value):
    for half in range(2):
        lo = max(0, HALF * half - RIM)
        hi = min(SIZE, HALF * half + HALF + RIM)
        for part in range(2):
            at = ((lo + RIM - HALF * half) * WIDE + col) * 8 + place(half, tile, part)
            grid[pl.ds(at, hi - lo, stride=WIDE * 8), :] = value[lo:hi, lanes_of(part)]


def fetch_strips(near_ids, own, slots, strips, near):
    def fetch(p, carry):
        t, d = p // 8, p % 8
        slot = near_ids[t, d]
        other = slot // 2
        s = slot - 2 * other
        off = lax.rem(other - own + slots // 2 + slots // 4, slots // 2) - slots // 4
        off = jnp.where(slot < 0, slots, off)

        @pl.when(slot < 0)
        def _():
            near[p] = jnp.zeros((RIM, SIZE, CH), F32)

        for strip, offset in zip(strips, OFFSETS):
            index = s if offset == 0 else 2 * s + t if abs(offset) == 1 else s + t

            @pl.when(off == offset)
            def _(strip=strip, index=index):
                near[p] = strip[index].astype(F32)

        return carry

    lax.fori_loop(0, 16, fetch, 0)


def load(sources, targets, sems):
    copies = [pltpu.make_async_copy(src, dst, sems.at[k]) for k, (src, dst) in enumerate(zip(sources, targets))]
    for copy in copies:
        copy.start()
    return copies


def wait_all(copies):
    for copy in copies:
        copy.wait()


def put_tiles(tile_ref, grid):
    for t in range(2):
        for i in range(SIZE):
            put_row(grid, WIDE, t, RIM + i, RIM, tile_ref[t, i].astype(F32))


def put_halo(near, grid):
    for t in range(2):
        for i in range(RIM):
            for row, mid, west, east in ((i, 0, 4, 5), (RIM + SIZE + i, 1, 6, 7)):
                put_row(grid, WIDE, t, row, 0, near[t * 8 + west, i, SIZE - RIM : SIZE, :])
                put_row(grid, WIDE, t, row, RIM, near[t * 8 + mid, i])
                put_row(grid, WIDE, t, row, RIM + SIZE, near[t * 8 + east, i, 0:RIM, :])
        for k in range(RIM):
            put_column(grid, t, k, near[t * 8 + 2, k])
            put_column(grid, t, RIM + SIZE + k, near[t * 8 + 3, k])


def pick_rim(near_ids, own, slots, s, offset, t):
    slot = lax.rem(2 * own + 2 * offset + t + slots, slots)
    rim = jnp.int32(0)
    for d in range(8):
        rim = jnp.where(near_ids[s, d] == slot, RIM_OF[d], rim)
    return 4 * s + rim


def send_strips(near_ids, own, slots, rims, outs, sems):
    copies = []
    for out, offset, pairs in zip(outs, OFFSETS, PAIRS):
        for k, (s, t) in enumerate(pairs):
            rim = rims.at[pick_rim(near_ids, own, slots, s, offset, t)]
            copies.append(pltpu.make_async_copy(rim, out.at[k], sems.at[len(copies)]))
            copies[-1].start()
    return copies


def spread_taps(kernel_ref, taps):
    even = lax.rem(lax.broadcasted_iota(jnp.int32, (8, 128), 0), 2) == 0
    for a in range(KW):
        for b in range(KW):
            low = jnp.broadcast_to(kernel_ref[a, b : b + 1, 0:128], (8, 128))
            high = jnp.broadcast_to(kernel_ref[a, b : b + 1, 128:256], (8, 128))
            taps[a * KW + b] = jnp.where(even, low, high)


def convolve(grid3, taps, flip, out3):
    def column(j, carry):
        acc = [None] * HALF
        for q in range(TAPS):
            tap = taps[TAPS - 1 - q if flip else q]
            for r in range(HALF):
                term = grid3[(r + q // KW) * WIDE + j + q % KW] * tap
                acc[r] = term if acc[r] is None else acc[r] + term
        for r in range(HALF):
            out3[r * SIZE + j] = acc[r]
        return carry

    lax.fori_loop(0, SIZE, column, 0)


def rows_of(flat, tile, half, r):
    return jnp.concatenate(
        [flat[pl.ds(r * SIZE * 8 + place(half, tile, part), SIZE, stride=8), :] for part in range(2)], axis=1
    )


def gelu_parts(x):
    size = jnp.abs(x)
    t = pl.reciprocal(1.0 + (0.3275911 * 0.7071067811865476) * size, approx=False)
    bell = jnp.exp2((-0.5 * 1.4426950408889634) * (x * x))
    poly = 0.5 * 1.061405429 * t - 0.5 * 1.453152027
    poly = poly * t + 0.5 * 1.421413741
    poly = poly * t - 0.5 * 0.284496736
    poly = poly * t + 0.5 * 0.254829592
    tail = poly * t * bell
    cdf = jnp.where(x < 0, tail, 1.0 - tail)
    return x * cdf, cdf + x * (bell * 0.3989422804014327)


def rim_kernel(own_ref, near_hbm, tile_hbm, *rest, slots):
    outs, (near_ids, tile_ref, rims, stage, sems, out_sems) = rest[:5], rest[5:]
    wait_all(load((near_hbm, tile_hbm), (near_ids, tile_ref), sems))
    for s in range(2):
        rims[4 * s] = tile_ref[s, 0:RIM]
        rims[4 * s + 1] = tile_ref[s, SIZE - RIM : SIZE]
        for side, first, row in ((2, 0, 0), (3, 16, 16 - RIM)):
            for part in range(2):
                stage[part] = tile_ref[s, :, first : first + 16, lanes_of(part)].astype(F32).reshape(SIZE * 16, 128)
                for k in range(RIM):
                    rims[4 * s + side, k, :, lanes_of(part)] = stage[part, pl.ds(row + k, SIZE, stride=16), :].astype(BF16)
    wait_all(send_strips(near_ids, own_ref[0], slots, rims, outs, out_sems))


def main_kernel(own_ref, near_hbm, h0, h1, h2, h3, h4, tile_hbm, kernel_hbm, gain_hbm, w_in_hbm, w_out_hbm, cot_hbm,
                share_hbm, grad_hbm, o0, o1, o2, o3, o4,
                near_ids, s0, s1, s2, s3, s4, tile_ref, kernel_ref, gain_ref, w_in_ref, w_out_ref, cot_ref,
                grid, near, taps, conv, gwi, gwo, rims, normed_ref, xhat_ref, inv_ref, gn_ref,
                acc, share_ref, grad_grid, grad_ref, sems, out_sems, strip_sems, *, slots):
    own = own_ref[0]
    copies = load(
        (tile_hbm, near_hbm, h0, h1, h2, h3, h4, kernel_hbm, gain_hbm, w_in_hbm, w_out_hbm, cot_hbm),
        (tile_ref, near_ids, s0, s1, s2, s3, s4, kernel_ref, gain_ref, w_in_ref, w_out_ref, cot_ref),
        sems,
    )
    copies[0].wait()
    put_tiles(tile_ref, grid)
    wait_all(copies[1:9])
    fetch_strips(near_ids, own, slots, (s0, s1, s2, s3, s4), near)
    spread_taps(kernel_ref, taps)
    put_halo(near, grid)
    grid3 = grid.reshape(TALL * WIDE, 8, 128)
    convolve(grid3, taps, False, conv.reshape(HALF * SIZE, 8, 128))
    gain = gain_ref[...]
    lines = ROWS // SIZE

    def where(n):
        return 0, place(n % 2, n // 2, 0)

    def normalise(n, carry):
        first, spot = where(n)
        cells = pl.ds(pl.multiple_of(n * ROWS, ROWS), ROWS)
        cv = jnp.concatenate(
            [
                jnp.concatenate(
                    [conv[pl.ds((first + r) * SIZE * 8 + spot + part, SIZE, stride=8), :] for part in range(2)], axis=1
                )
                for r in range(lines)
            ],
            axis=0,
        )
        cv = cv - jnp.mean(cv, axis=-1, keepdims=True)
        inv = lax.rsqrt(jnp.mean(cv * cv, axis=-1, keepdims=True) + 1e-06)
        xhat = cv * inv
        xhat_ref[cells, :] = xhat
        inv_ref[cells, :] = jnp.broadcast_to(inv, (ROWS, 128))
        normed_ref[cells, :] = (xhat * gain).astype(BF16)
        return carry

    lax.fori_loop(0, 2 * SIZE * SIZE // ROWS, normalise, 0)
    wait_all(copies[9:])
    steps = [(t, slice(f * 256, f * 256 + 256)) for t in range(2) for f in range(FF // 256)]
    cells_of = [slice(t * SIZE * SIZE, (t + 1) * SIZE * SIZE) for t in range(2)]
    across = (((1,), (1,)), ((), ()))

    def forward(step):
        t, cols = step
        pre = jnp.dot(normed_ref[cells_of[t], :], w_in_ref[:, cols], preferred_element_type=F32)
        return pre, lax.dot_general(cot_ref[cells_of[t], :], w_out_ref[cols, :], across, preferred_element_type=F32)

    ahead = forward(steps[0])
    for k, (t, cols) in enumerate(steps):
        pre, gact = ahead
        if k + 1 < len(steps):
            ahead = forward(steps[k + 1])
        if cols.start == 0:
            normed_t = normed_ref[cells_of[t], :].T
            cot_t = cot_ref[cells_of[t], :].T
        act, slope = gelu_parts(pre)
        act = act.astype(BF16)
        gpre = (gact * slope).astype(BF16)
        one = jnp.dot(normed_t, gpre, preferred_element_type=F32)
        two = jnp.dot(cot_t, act, preferred_element_type=F32)
        gn = lax.dot_general(gpre, w_in_ref[:, cols], across, preferred_element_type=F32)
        if t == 0:
            gwi[:, cols] = one
            gwo[:, cols] = two
        else:
            gwi[:, cols] += one
            gwo[:, cols] += two
        if cols.start == 0:
            gn_ref[cells_of[t], :] = gn
        else:
            gn_ref[cells_of[t], :] += gn

    def denormalise(n, ggain):
        first, spot = where(n)
        cells = pl.ds(pl.multiple_of(n * ROWS, ROWS), ROWS)
        gn, xhat = gn_ref[cells, :], xhat_ref[cells, :]
        inv = inv_ref[cells, 0:1]
        ggain = ggain + jnp.sum((gn * xhat).reshape(ROWS // 8, 8, CH), axis=0)
        gx = gn * gain
        m1 = jnp.mean(gx, axis=-1, keepdims=True)
        m2 = jnp.mean(gx * xhat, axis=-1, keepdims=True)
        gc = (inv * (gx - m1 - xhat * m2)).astype(BF16)
        grad_ref[cells, :] = gc
        gc = gc.astype(F32)
        for r in range(lines):
            piece = gc[r * SIZE : (r + 1) * SIZE]
            at = ((first + r + RIM) * WIDE + RIM) * 8 + spot
            for part in range(2):
                grad_grid[pl.ds(at + part, SIZE, stride=8), :] = piece[:, lanes_of(part)]
        return ggain

    ggain = lax.fori_loop(0, 2 * SIZE * SIZE // ROWS, denormalise, jnp.zeros((8, CH), F32))
    results = [pltpu.make_async_copy(grad_ref, grad_hbm, out_sems.at[0])]
    results[0].start()

    def send_rows(first, count, sem):
        for k in range(NEAR_GROUP):
            rows = pl.ds(PIECE * k + first, count)
            results.append(pltpu.make_async_copy(share_ref.at[:, rows], share_hbm.at[:, rows], out_sems.at[sem + k]))
            results[-1].start()

    low = lax.broadcasted_iota(jnp.int32, (CH, 128), 1) < 64
    for p in range(FF // 128):
        one = gwi[:, p * 128 : p * 128 + 128]
        two = gwo[:, p * 128 : p * 128 + 128]
        even = jnp.where(low, one, pltpu.roll(two, 64, 1)).astype(BF16)
        odd = jnp.where(low, pltpu.roll(one, 64, 1), two).astype(BF16)
        for k in range(NEAR_GROUP):
            share_ref[2 * p, PIECE * k : PIECE * k + 32] = even[32 * k : 32 * k + 32]
            share_ref[2 * p + 1, PIECE * k : PIECE * k + 32] = odd[32 * k : 32 * k + 32]
    send_rows(0, 32, 1)
    tap_gradients(grid3, grad_grid.reshape(TALL * WIDE, 8, 128), ggain, acc, share_ref)
    send_rows(32, 16, 1 + NEAR_GROUP)
    for t in range(2):
        for part in range(2):
            lanes = lanes_of(part)
            for k in range(RIM):
                top = ((RIM + k) * WIDE + RIM) * 8 + place(0, t, part)
                bottom = ((HALF + k) * WIDE + RIM) * 8 + place(1, t, part)
                rims[4 * t, k, :, lanes] = grad_grid[pl.ds(top, SIZE, stride=8), :].astype(BF16)
                rims[4 * t + 1, k, :, lanes] = grad_grid[pl.ds(bottom, SIZE, stride=8), :].astype(BF16)
                for side, col in ((2, RIM + k), (3, SIZE + k)):
                    both = [
                        grad_grid[pl.ds((RIM * WIDE + col) * 8 + place(half, t, part), HALF, stride=WIDE * 8), :]
                        for half in range(2)
                    ]
                    rims[4 * t + side, k, :, lanes] = jnp.concatenate(both, axis=0).astype(BF16)
    wait_all(results + send_strips(near_ids, own, slots, rims, (o0, o1, o2, o3, o4), strip_sems))


def tap_gradients(grid3, grad3, ggain, acc, share_ref):
    acc[...] = jnp.zeros_like(acc)

    def column(j, carry):
        g = [grad3[(RIM + r) * WIDE + RIM + j] for r in range(HALF)]
        for q in range(TAPS):
            terms = [grid3[(r + q // KW) * WIDE + j + q % KW] * g[r] for r in range(HALF)]
            while len(terms) > 1:
                terms = [terms[k] + terms[k + 1] for k in range(0, len(terms), 2)]
            acc[q] += terms[0]
        return carry

    lax.fori_loop(0, SIZE, column, 0)
    even = lax.rem(lax.broadcasted_iota(jnp.int32, (8, 128), 0), 2) == 0
    sums = [[], []]
    for q in range(TAPS):
        one = acc[q]
        sums[0].append(jnp.sum(jnp.where(even, one, 0.0), axis=0, keepdims=True))
        sums[1].append(jnp.sum(jnp.where(even, 0.0, one), axis=0, keepdims=True))
    for part in range(2):
        sums[part].append(jnp.sum(ggain[:, lanes_of(part)], axis=0, keepdims=True))
        sums[part].append(jnp.zeros((PART_ROWS - TAPS - 1, 128), F32))
    total = jnp.concatenate(sums[0] + sums[1], axis=0).astype(BF16)
    for d in range(16):
        for k in range(NEAR_GROUP):
            share_ref[d, PIECE * k + 32 : PIECE * k + 48] = total[16 * k : 16 * k + 16]


def back_kernel(own_ref, near_hbm, h0, h1, h2, h3, h4, grad_hbm, kernel_hbm, cot_hbm, out_ref,
                near_ids, s0, s1, s2, s3, s4, grad_ref, kernel_ref, cot_ref, grid, near, taps, conv, sems, *, slots):
    copies = load(
        (grad_hbm, near_hbm, h0, h1, h2, h3, h4, kernel_hbm, cot_hbm),
        (grad_ref, near_ids, s0, s1, s2, s3, s4, kernel_ref, cot_ref),
        sems,
    )
    copies[0].wait()
    put_tiles(grad_ref, grid)
    wait_all(copies[1:])
    fetch_strips(near_ids, own_ref[0], slots, (s0, s1, s2, s3, s4), near)
    spread_taps(kernel_ref, taps)
    put_halo(near, grid)
    convolve(grid.reshape(TALL * WIDE, 8, 128), taps, True, conv.reshape(HALF * SIZE, 8, 128))
    for t in range(2):
        for i in range(SIZE):
            out_ref[t, i] = (cot_ref[t, i].astype(F32) + rows_of(conv, t, i // HALF, i % HALF)).astype(BF16)


def sum_kernel(in_ref, out_ref):
    out_ref[...] = jnp.sum(in_ref[...].astype(F32), axis=0).astype(BF16)


def last_kernel(in_ref, w_in_ref, w_out_ref, taps_ref, gain_ref, low, *, scale):
    weights = (in_ref[:, 0:32, :].astype(F32) * scale).reshape(CH, 128).T
    w_in_ref[...] = weights[0:64, :]
    w_out_ref[...] = weights[64:128, :]
    low[...] = (in_ref[:, 32:48, :].astype(F32) * scale).reshape(2 * PART_ROWS, 128)
    for part in range(2):
        lanes = lanes_of(part)
        for a in range(KW):
            at = part * PART_ROWS + a * KW
            taps_ref[a, :, lanes] = low[at : at + KW, :]
        at = part * PART_ROWS + TAPS
        gain_ref[:, lanes] = low[at : at + 1, :]


SMEM = pl.BlockSpec(memory_space=pltpu.SMEM)
STRIPS = tuple(jax.ShapeDtypeStruct((n, RIM, SIZE, CH), BF16) for n in COUNTS)
RIMS = pltpu.VMEM((8, RIM, SIZE, CH), BF16)
NEAR = pltpu.VMEM((16, RIM, SIZE, CH), F32)
GRID = jax.ShapeDtypeStruct((TALL * WIDE * 8, 128), F32)
GRID_SPACE = pltpu.VMEM(GRID.shape, F32)
SPREAD = pltpu.VMEM((TAPS, 8, 128), F32)
CELLS = 2 * SIZE * SIZE
SHARE = jax.ShapeDtypeStruct((16, NEAR_GROUP * PIECE, 128), BF16)
CONV = pltpu.VMEM((HALF * SIZE * 8, 128), F32)


STRIP_SEMS = pltpu.SemaphoreType.DMA((sum(COUNTS),))
IDS = pltpu.SMEM((2, 8), jnp.int32)
TILES = pltpu.VMEM((2, SIZE, SIZE, CH), BF16)
LANDED = (IDS, *(pltpu.VMEM(x.shape, BF16) for x in STRIPS), TILES, pltpu.VMEM((KW, KW, CH), F32))
MAIN_SCRATCH = (
    *LANDED,
    pltpu.VMEM((1, CH), F32),
    pltpu.VMEM((CH, FF), BF16),
    pltpu.VMEM((FF, CH), BF16),
    pltpu.VMEM((CELLS, CH), BF16),
    GRID_SPACE,
    NEAR,
    SPREAD,
    CONV,
    pltpu.VMEM((CH, FF), F32),
    pltpu.VMEM((CH, FF), F32),
    RIMS,
    pltpu.VMEM((CELLS, CH), BF16),
    pltpu.VMEM((CELLS, CH), F32),
    pltpu.VMEM((CELLS, 128), F32),
    pltpu.VMEM((CELLS, CH), F32),
    SPREAD,
    pltpu.VMEM(SHARE.shape, BF16),
    GRID_SPACE,
    pltpu.VMEM((CELLS, CH), BF16),
    pltpu.SemaphoreType.DMA((12,)),
    pltpu.SemaphoreType.DMA((1 + 2 * NEAR_GROUP,)),
    STRIP_SEMS,
)


def call(kernel, name, out, scalars, arrays, scratch=(), far=(), far_outs=0, flops=10**6, moved=10**6, vmem_mib=24):
    vmem = pl.BlockSpec(memory_space=pltpu.VMEM)
    hbm = pl.BlockSpec(memory_space=pltpu.HBM)
    return pl.pallas_call(
        kernel,
        out_shape=out,
        in_specs=[SMEM] * len(scalars) + [vmem] * len(arrays) + [hbm] * len(far),
        out_specs=[hbm] * far_outs + [vmem] * (len(out) - far_outs) if isinstance(out, tuple) else vmem,
        scratch_shapes=scratch,
        compiler_params=pltpu.CompilerParams(vmem_limit_bytes=vmem_mib * 1024 * 1024),
        cost_estimate=pl.CostEstimate(flops=flops, bytes_accessed=moved, transcendentals=0),
        name=name,
    )(*scalars, *arrays, *far)


def exchange(strips):
    n = lax.axis_size("tiles")
    got = {0: strips[0]}
    for off, strip in zip(OFFSETS[1:], strips[1:]):
        got[-off] = lax.ppermute(strip, "tiles", [(i, (i + off) % n) for i in range(n)])
    return tuple(got[off] for off in OFFSETS)


def sum_of(pieces):
    return jnp.sum(pieces.astype(F32), axis=0)


def copies_of(piece, count):
    return jnp.broadcast_to(piece[None], (count, *piece.shape))


def group_exchange(pieces, groups):
    return lax.all_to_all(pieces, "tiles", 0, 0, tiled=True, axis_index_groups=groups)


def body(fields, neighbours, kernel, gain, w_in, w_out, cotangent):
    n_tiles, n_dp = lax.axis_size("tiles"), lax.axis_size("dp")
    slots = 2 * n_tiles
    own = (lax.axis_index("tiles").reshape(1).astype(jnp.int32),)
    tiles, cot = fields[0], cotangent[0]
    stage = pltpu.VMEM((2, SIZE * 16, 128), F32)
    sent = call(
        functools.partial(rim_kernel, slots=slots),
        "rims",
        STRIPS,
        own,
        (),
        (IDS, TILES, RIMS, stage, pltpu.SemaphoreType.DMA((2,)), STRIP_SEMS),
        far=(neighbours, tiles),
        far_outs=5,
        vmem_mib=60,
    )
    got = exchange(sent)
    share, grad, *sent = call(
        functools.partial(main_kernel, slots=slots),
        "main",
        (SHARE, jax.ShapeDtypeStruct((CELLS, CH), BF16), *STRIPS),
        own,
        (),
        MAIN_SCRATCH,
        far=(neighbours, *got, tiles, kernel, gain.reshape(1, CH), w_in, w_out, cot.reshape(CELLS, CH)),
        far_outs=7,
        flops=40 * 10**9,
        vmem_mib=60,
    )
    share = lax.all_to_all(share, "dp", 0, 0, tiled=True)
    share, got = lax.optimization_barrier((share, exchange(sent)))
    grad_fields = call(
        functools.partial(back_kernel, slots=slots),
        "back",
        jax.ShapeDtypeStruct((2, SIZE, SIZE, CH), BF16),
        own,
        (),
        (*LANDED, TILES, GRID_SPACE, NEAR, SPREAD, CONV, pltpu.SemaphoreType.DMA((9,))),
        far=(neighbours, *got, grad.reshape(tiles.shape), kernel, cot),
        flops=12 * 10**9,
        vmem_mib=60,
    )
    cut = call(sum_kernel, "sum_dp", jax.ShapeDtypeStruct(SHARE.shape[1:], BF16), (), (share,), vmem_mib=16)
    near = [list(range(g, g + NEAR_GROUP)) for g in range(0, n_tiles, NEAR_GROUP)]
    far = [list(range(g, n_tiles, NEAR_GROUP)) for g in range(NEAR_GROUP)]
    cut = group_exchange(cut.reshape(NEAR_GROUP, PIECE, 128), near)
    cut = group_exchange(copies_of(sum_of(cut), len(far[0])), far)
    cut, grad_fields = lax.optimization_barrier((cut, grad_fields))
    cut = group_exchange(copies_of(sum_of(cut).astype(BF16), NEAR_GROUP), near)
    scale = float((n_dp * slots * SIZE * SIZE) ** -0.5)
    g_in, g_out, g_taps, g_gain = call(
        functools.partial(last_kernel, scale=scale),
        "last",
        (
            jax.ShapeDtypeStruct((64, CH), F32),
            jax.ShapeDtypeStruct((64, CH), F32),
            jax.ShapeDtypeStruct((KW, KW, CH), F32),
            jax.ShapeDtypeStruct((1, CH), F32),
        ),
        (),
        (cut,),
        (pltpu.VMEM((2 * PART_ROWS, 128), F32),),
    )
    return grad_fields[None], g_in.T, g_out, g_taps, g_gain.reshape(CH)


def solution(mesh):
    return jax.shard_map(
        body,
        mesh=mesh,
        in_specs=(
            P("dp", "tiles", None, None, None),
            P("tiles", None),
            P(),
            P(),
            P(),
            P(),
            P("dp", "tiles", None, None, None),
        ),
        out_specs=(P("dp", "tiles", None, None, None), P(None, "dp"), P("dp", None), P(), P()),
        check_vma=False,
    )
```

```python
import functools

import jax
import jax.numpy as jnp
from jax import lax
from jax.experimental import pallas as pl
from jax.experimental.pallas import tpu as pltpu
from jax.sharding import PartitionSpec as P

KW = 7
TAPS = KW * KW
RIM = KW // 2
SIZE = 32
WIDE = SIZE + 2 * RIM
HALF = SIZE // 2
TALL = HALF + 2 * RIM
CH = 256
FF = 1024
NEAR_GROUP = 8
PIECE = 48
PART_ROWS = 64
ROWS = 512
F32 = jnp.float32
BF16 = jnp.bfloat16
OFFSETS = (0, -1, 1, -2, 2)
PAIRS = (
    ((0, 1), (1, 0)),
    ((0, 0), (0, 1), (1, 0), (1, 1)),
    ((0, 0), (0, 1), (1, 0), (1, 1)),
    ((0, 0), (0, 1), (1, 1)),
    ((0, 0), (1, 0), (1, 1)),
)
COUNTS = tuple(len(p) for p in PAIRS)
RIM_OF = (0, 1, 2, 3, 0, 0, 1, 1)


def place(half, tile, part):
    return 4 * half + 2 * tile + part


def lanes_of(part):
    return slice(part * 128, part * 128 + 128)


def put_row(grid, pitch, tile, row, first, value):
    count = value.shape[0]
    for half in range(2):
        i = row - HALF * half
        if 0 <= i < TALL:
            for part in range(2):
                at = (i * pitch + first) * 8 + place(half, tile, part)
                grid[pl.ds(at, count, stride=8), :] = value[:, lanes_of(part)]


def put_column(grid, tile, col, value):
    for half in range(2):
        lo = max(0, HALF * half - RIM)
        hi = min(SIZE, HALF * half + HALF + RIM)
        for part in range(2):
            at = ((lo + RIM - HALF * half) * WIDE + col) * 8 + place(half, tile, part)
            grid[pl.ds(at, hi - lo, stride=WIDE * 8), :] = value[lo:hi, lanes_of(part)]


def fetch_strips(near_ids, own, slots, strips, near):
    def fetch(p, carry):
        t, d = p // 8, p % 8
        slot = near_ids[t, d]
        other = slot // 2
        s = slot - 2 * other
        off = lax.rem(other - own + slots // 2 + slots // 4, slots // 2) - slots // 4
        off = jnp.where(slot < 0, slots, off)

        @pl.when(slot < 0)
        def _():
            near[p] = jnp.zeros((RIM, SIZE, CH), F32)

        for strip, offset in zip(strips, OFFSETS):
            index = s if offset == 0 else 2 * s + t if abs(offset) == 1 else s + t

            @pl.when(off == offset)
            def _(strip=strip, index=index):
                near[p] = strip[index].astype(F32)

        return carry

    lax.fori_loop(0, 16, fetch, 0)


def load(sources, targets, sems):
    copies = [pltpu.make_async_copy(src, dst, sems.at[k]) for k, (src, dst) in enumerate(zip(sources, targets))]
    for copy in copies:
        copy.start()
    return copies


def wait_all(copies):
    for copy in copies:
        copy.wait()


def put_tiles(tile_ref, grid):
    for t in range(2):
        for i in range(SIZE):
            put_row(grid, WIDE, t, RIM + i, RIM, tile_ref[t, i].astype(F32))


def put_halo(near, grid):
    for t in range(2):
        for i in range(RIM):
            for row, mid, west, east in ((i, 0, 4, 5), (RIM + SIZE + i, 1, 6, 7)):
                put_row(grid, WIDE, t, row, 0, near[t * 8 + west, i, SIZE - RIM : SIZE, :])
                put_row(grid, WIDE, t, row, RIM, near[t * 8 + mid, i])
                put_row(grid, WIDE, t, row, RIM + SIZE, near[t * 8 + east, i, 0:RIM, :])
        for k in range(RIM):
            put_column(grid, t, k, near[t * 8 + 2, k])
            put_column(grid, t, RIM + SIZE + k, near[t * 8 + 3, k])


def pick_rim(near_ids, own, slots, s, offset, t):
    slot = lax.rem(2 * own + 2 * offset + t + slots, slots)
    rim = jnp.int32(0)
    for d in range(8):
        rim = jnp.where(near_ids[s, d] == slot, RIM_OF[d], rim)
    return 4 * s + rim


def send_strips(near_ids, own, slots, rims, outs, sems):
    copies = []
    for out, offset, pairs in zip(outs, OFFSETS, PAIRS):
        for k, (s, t) in enumerate(pairs):
            rim = rims.at[pick_rim(near_ids, own, slots, s, offset, t)]
            copies.append(pltpu.make_async_copy(rim, out.at[k], sems.at[len(copies)]))
            copies[-1].start()
    return copies


def spread_taps(kernel_ref, taps):
    even = lax.rem(lax.broadcasted_iota(jnp.int32, (8, 128), 0), 2) == 0
    for a in range(KW):
        for b in range(KW):
            low = jnp.broadcast_to(kernel_ref[a, b : b + 1, 0:128], (8, 128))
            high = jnp.broadcast_to(kernel_ref[a, b : b + 1, 128:256], (8, 128))
            taps[a * KW + b] = jnp.where(even, low, high)


def convolve(grid3, taps, flip, out3):
    def column(j, carry):
        acc = [None] * HALF
        for q in range(TAPS):
            tap = taps[TAPS - 1 - q if flip else q]
            for r in range(HALF):
                term = grid3[(r + q // KW) * WIDE + j + q % KW] * tap
                acc[r] = term if acc[r] is None else acc[r] + term
        for r in range(HALF):
            out3[r * SIZE + j] = acc[r]
        return carry

    lax.fori_loop(0, SIZE, column, 0)


def rows_of(flat, tile, half, r):
    return jnp.concatenate(
        [flat[pl.ds(r * SIZE * 8 + place(half, tile, part), SIZE, stride=8), :] for part in range(2)], axis=1
    )


def gelu_parts(x):
    size = jnp.abs(x)
    t = pl.reciprocal(1.0 + (0.3275911 * 0.7071067811865476) * size, approx=False)
    bell = jnp.exp2((-0.5 * 1.4426950408889634) * (x * x))
    poly = 0.5 * 1.061405429 * t - 0.5 * 1.453152027
    poly = poly * t + 0.5 * 1.421413741
    poly = poly * t - 0.5 * 0.284496736
    poly = poly * t + 0.5 * 0.254829592
    tail = poly * t * bell
    cdf = jnp.where(x < 0, tail, 1.0 - tail)
    return x * cdf, cdf + x * (bell * 0.3989422804014327)


def rim_kernel(own_ref, near_hbm, tile_hbm, *rest, slots):
    outs, (near_ids, tile_ref, rims, stage, sems, out_sems) = rest[:5], rest[5:]
    copies = load((near_hbm, tile_hbm.at[0], tile_hbm.at[1]), (near_ids, tile_ref.at[0], tile_ref.at[1]), sems)
    copies[0].wait()
    for s in range(2):
        copies[1 + s].wait()
        rims[4 * s] = tile_ref[s, 0:RIM]
        rims[4 * s + 1] = tile_ref[s, SIZE - RIM : SIZE]
        for side, first, row in ((2, 0, 0), (3, 16, 16 - RIM)):
            for part in range(2):
                stage[part] = tile_ref[s, :, first : first + 16, lanes_of(part)].astype(F32).reshape(SIZE * 16, 128)
                for k in range(RIM):
                    rims[4 * s + side, k, :, lanes_of(part)] = stage[part, pl.ds(row + k, SIZE, stride=16), :].astype(BF16)
    wait_all(send_strips(near_ids, own_ref[0], slots, rims, outs, out_sems))


def main_kernel(own_ref, near_hbm, h0, h1, h2, h3, h4, tile_hbm, kernel_hbm, gain_hbm, w_in_hbm, w_out_hbm, cot_hbm,
                share_hbm, grad_hbm, o0, o1, o2, o3, o4,
                near_ids, s0, s1, s2, s3, s4, tile_ref, kernel_ref, gain_ref, w_in_ref, w_out_ref, cot_ref,
                grid, near, taps, conv, gwi, gwo, rims, normed_ref, xhat_ref, inv_ref, gn_ref,
                acc, share_ref, grad_grid, grad_ref, sems, out_sems, strip_sems, *, slots):
    own = own_ref[0]
    copies = load(
        (tile_hbm, near_hbm, h0, h1, h2, h3, h4, kernel_hbm, gain_hbm, w_in_hbm, w_out_hbm, cot_hbm),
        (tile_ref, near_ids, s0, s1, s2, s3, s4, kernel_ref, gain_ref, w_in_ref, w_out_ref, cot_ref),
        sems,
    )
    copies[0].wait()
    put_tiles(tile_ref, grid)
    wait_all(copies[1:9])
    fetch_strips(near_ids, own, slots, (s0, s1, s2, s3, s4), near)
    spread_taps(kernel_ref, taps)
    put_halo(near, grid)
    grid3 = grid.reshape(TALL * WIDE, 8, 128)
    convolve(grid3, taps, False, conv.reshape(HALF * SIZE, 8, 128))
    gain = gain_ref[...]
    lines = ROWS // SIZE

    def where(n):
        return 0, place(n % 2, n // 2, 0)

    def normalise(n, carry):
        first, spot = where(n)
        cells = pl.ds(pl.multiple_of(n * ROWS, ROWS), ROWS)
        cv = jnp.concatenate(
            [
                jnp.concatenate(
                    [conv[pl.ds((first + r) * SIZE * 8 + spot + part, SIZE, stride=8), :] for part in range(2)], axis=1
                )
                for r in range(lines)
            ],
            axis=0,
        )
        cv = cv - jnp.mean(cv, axis=-1, keepdims=True)
        inv = lax.rsqrt(jnp.mean(cv * cv, axis=-1, keepdims=True) + 1e-06)
        xhat = cv * inv
        xhat_ref[cells, :] = xhat
        inv_ref[cells, :] = jnp.broadcast_to(inv, (ROWS, 128))
        normed_ref[cells, :] = (xhat * gain).astype(BF16)
        return carry

    lax.fori_loop(0, 2 * SIZE * SIZE // ROWS, normalise, 0, unroll=True)
    wait_all(copies[9:])
    steps = [(t, slice(f * 256, f * 256 + 256)) for t in range(2) for f in range(FF // 256)]
    cells_of = [slice(t * SIZE * SIZE, (t + 1) * SIZE * SIZE) for t in range(2)]
    across = (((1,), (1,)), ((), ()))

    def forward(step):
        t, cols = step
        pre = jnp.dot(normed_ref[cells_of[t], :], w_in_ref[:, cols], preferred_element_type=F32)
        return pre, lax.dot_general(cot_ref[cells_of[t], :], w_out_ref[cols, :], across, preferred_element_type=F32)

    ahead = forward(steps[0])
    for k, (t, cols) in enumerate(steps):
        pre, gact = ahead
        if k + 1 < len(steps):
            ahead = forward(steps[k + 1])
        if cols.start == 0:
            normed_t = normed_ref[cells_of[t], :].T
            cot_t = cot_ref[cells_of[t], :].T
        act, slope = gelu_parts(pre)
        act = act.astype(BF16)
        gpre = (gact * slope).astype(BF16)
        one = jnp.dot(normed_t, gpre, preferred_element_type=F32)
        two = jnp.dot(cot_t, act, preferred_element_type=F32)
        gn = lax.dot_general(gpre, w_in_ref[:, cols], across, preferred_element_type=F32)
        if t == 0:
            gwi[:, cols] = one
            gwo[:, cols] = two
        else:
            gwi[:, cols] += one
            gwo[:, cols] += two
        if cols.start == 0:
            gn_ref[cells_of[t], :] = gn
        else:
            gn_ref[cells_of[t], :] += gn

    def denormalise(n, ggain):
        first, spot = where(n)
        cells = pl.ds(pl.multiple_of(n * ROWS, ROWS), ROWS)
        gn, xhat = gn_ref[cells, :], xhat_ref[cells, :]
        inv = inv_ref[cells, 0:1]
        ggain = ggain + jnp.sum((gn * xhat).reshape(ROWS // 8, 8, CH), axis=0)
        gx = gn * gain
        m1 = jnp.mean(gx, axis=-1, keepdims=True)
        m2 = jnp.mean(gx * xhat, axis=-1, keepdims=True)
        gc = (inv * (gx - m1 - xhat * m2)).astype(BF16)
        grad_ref[cells, :] = gc
        gc = gc.astype(F32)
        for r in range(lines):
            piece = gc[r * SIZE : (r + 1) * SIZE]
            at = ((first + r + RIM) * WIDE + RIM) * 8 + spot
            for part in range(2):
                grad_grid[pl.ds(at + part, SIZE, stride=8), :] = piece[:, lanes_of(part)]
        return ggain

    ggain = lax.fori_loop(0, 2 * SIZE * SIZE // ROWS, denormalise, jnp.zeros((8, CH), F32), unroll=True)
    results = [pltpu.make_async_copy(grad_ref, grad_hbm, out_sems.at[0])]
    results[0].start()

    def send_rows(first, count, sem):
        for k in range(NEAR_GROUP):
            rows = pl.ds(PIECE * k + first, count)
            results.append(pltpu.make_async_copy(share_ref.at[:, rows], share_hbm.at[:, rows], out_sems.at[sem + k]))
            results[-1].start()

    low = lax.broadcasted_iota(jnp.int32, (CH, 128), 1) < 64
    for p in range(FF // 128):
        one = gwi[:, p * 128 : p * 128 + 128]
        two = gwo[:, p * 128 : p * 128 + 128]
        even = jnp.where(low, one, pltpu.roll(two, 64, 1)).astype(BF16)
        odd = jnp.where(low, pltpu.roll(one, 64, 1), two).astype(BF16)
        for k in range(NEAR_GROUP):
            share_ref[2 * p, PIECE * k : PIECE * k + 32] = even[32 * k : 32 * k + 32]
            share_ref[2 * p + 1, PIECE * k : PIECE * k + 32] = odd[32 * k : 32 * k + 32]
    send_rows(0, 32, 1)
    tap_gradients(grid3, grad_grid.reshape(TALL * WIDE, 8, 128), ggain, acc, share_ref)
    send_rows(32, 16, 1 + NEAR_GROUP)
    for t in range(2):
        for part in range(2):
            lanes = lanes_of(part)
            for k in range(RIM):
                top = ((RIM + k) * WIDE + RIM) * 8 + place(0, t, part)
                bottom = ((HALF + k) * WIDE + RIM) * 8 + place(1, t, part)
                rims[4 * t, k, :, lanes] = grad_grid[pl.ds(top, SIZE, stride=8), :].astype(BF16)
                rims[4 * t + 1, k, :, lanes] = grad_grid[pl.ds(bottom, SIZE, stride=8), :].astype(BF16)
                for side, col in ((2, RIM + k), (3, SIZE + k)):
                    both = [
                        grad_grid[pl.ds((RIM * WIDE + col) * 8 + place(half, t, part), HALF, stride=WIDE * 8), :]
                        for half in range(2)
                    ]
                    rims[4 * t + side, k, :, lanes] = jnp.concatenate(both, axis=0).astype(BF16)
    wait_all(results + send_strips(near_ids, own, slots, rims, (o0, o1, o2, o3, o4), strip_sems))


def tap_gradients(grid3, grad3, ggain, acc, share_ref):
    acc[...] = jnp.zeros_like(acc)

    def column(j, carry):
        g = [grad3[(RIM + r) * WIDE + RIM + j] for r in range(HALF)]
        for q in range(TAPS):
            terms = [grid3[(r + q // KW) * WIDE + j + q % KW] * g[r] for r in range(HALF)]
            while len(terms) > 1:
                terms = [terms[k] + terms[k + 1] for k in range(0, len(terms), 2)]
            acc[q] += terms[0]
        return carry

    lax.fori_loop(0, SIZE, column, 0)
    even = lax.rem(lax.broadcasted_iota(jnp.int32, (8, 128), 0), 2) == 0
    sums = [[], []]
    for q in range(TAPS):
        one = acc[q]
        sums[0].append(jnp.sum(jnp.where(even, one, 0.0), axis=0, keepdims=True))
        sums[1].append(jnp.sum(jnp.where(even, 0.0, one), axis=0, keepdims=True))
    for part in range(2):
        sums[part].append(jnp.sum(ggain[:, lanes_of(part)], axis=0, keepdims=True))
        sums[part].append(jnp.zeros((PART_ROWS - TAPS - 1, 128), F32))
    total = jnp.concatenate(sums[0] + sums[1], axis=0).astype(BF16)
    for d in range(16):
        for k in range(NEAR_GROUP):
            share_ref[d, PIECE * k + 32 : PIECE * k + 48] = total[16 * k : 16 * k + 16]


def back_kernel(own_ref, near_hbm, h0, h1, h2, h3, h4, grad_hbm, kernel_hbm, cot_hbm, out_ref,
                near_ids, s0, s1, s2, s3, s4, grad_ref, kernel_ref, cot_ref, grid, near, taps, conv, sems, *, slots):
    copies = load(
        (grad_hbm, near_hbm, h0, h1, h2, h3, h4, kernel_hbm, cot_hbm),
        (grad_ref, near_ids, s0, s1, s2, s3, s4, kernel_ref, cot_ref),
        sems,
    )
    copies[0].wait()
    put_tiles(grad_ref, grid)
    wait_all(copies[1:])
    fetch_strips(near_ids, own_ref[0], slots, (s0, s1, s2, s3, s4), near)
    spread_taps(kernel_ref, taps)
    put_halo(near, grid)
    convolve(grid.reshape(TALL * WIDE, 8, 128), taps, True, conv.reshape(HALF * SIZE, 8, 128))
    for t in range(2):
        for i in range(SIZE):
            out_ref[t, i] = (cot_ref[t, i].astype(F32) + rows_of(conv, t, i // HALF, i % HALF)).astype(BF16)


def sum_kernel(in_ref, out_ref):
    out_ref[...] = jnp.sum(in_ref[...].astype(F32), axis=0).astype(BF16)


def last_kernel(in_ref, w_in_ref, w_out_ref, taps_ref, gain_ref, low, *, scale):
    weights = (in_ref[:, 0:32, :].astype(F32) * scale).reshape(CH, 128).T
    w_in_ref[...] = weights[0:64, :]
    w_out_ref[...] = weights[64:128, :]
    low[...] = (in_ref[:, 32:48, :].astype(F32) * scale).reshape(2 * PART_ROWS, 128)
    for part in range(2):
        lanes = lanes_of(part)
        for a in range(KW):
            at = part * PART_ROWS + a * KW
            taps_ref[a, :, lanes] = low[at : at + KW, :]
        at = part * PART_ROWS + TAPS
        gain_ref[:, lanes] = low[at : at + 1, :]


SMEM = pl.BlockSpec(memory_space=pltpu.SMEM)
STRIPS = tuple(jax.ShapeDtypeStruct((n, RIM, SIZE, CH), BF16) for n in COUNTS)
RIMS = pltpu.VMEM((8, RIM, SIZE, CH), BF16)
NEAR = pltpu.VMEM((16, RIM, SIZE, CH), F32)
GRID = jax.ShapeDtypeStruct((TALL * WIDE * 8, 128), F32)
GRID_SPACE = pltpu.VMEM(GRID.shape, F32)
SPREAD = pltpu.VMEM((TAPS, 8, 128), F32)
CELLS = 2 * SIZE * SIZE
SHARE = jax.ShapeDtypeStruct((16, NEAR_GROUP * PIECE, 128), BF16)
CONV = pltpu.VMEM((HALF * SIZE * 8, 128), F32)


STRIP_SEMS = pltpu.SemaphoreType.DMA((sum(COUNTS),))
IDS = pltpu.SMEM((2, 8), jnp.int32)
TILES = pltpu.VMEM((2, SIZE, SIZE, CH), BF16)
LANDED = (IDS, *(pltpu.VMEM(x.shape, BF16) for x in STRIPS), TILES, pltpu.VMEM((KW, KW, CH), F32))
MAIN_SCRATCH = (
    *LANDED,
    pltpu.VMEM((1, CH), F32),
    pltpu.VMEM((CH, FF), BF16),
    pltpu.VMEM((FF, CH), BF16),
    pltpu.VMEM((CELLS, CH), BF16),
    GRID_SPACE,
    NEAR,
    SPREAD,
    CONV,
    pltpu.VMEM((CH, FF), F32),
    pltpu.VMEM((CH, FF), F32),
    RIMS,
    pltpu.VMEM((CELLS, CH), BF16),
    pltpu.VMEM((CELLS, CH), F32),
    pltpu.VMEM((CELLS, 128), F32),
    pltpu.VMEM((CELLS, CH), F32),
    SPREAD,
    pltpu.VMEM(SHARE.shape, BF16),
    GRID_SPACE,
    pltpu.VMEM((CELLS, CH), BF16),
    pltpu.SemaphoreType.DMA((12,)),
    pltpu.SemaphoreType.DMA((1 + 2 * NEAR_GROUP,)),
    STRIP_SEMS,
)


def call(kernel, name, out, scalars, arrays, scratch=(), far=(), far_outs=0, flops=10**6, moved=10**6, vmem_mib=24):
    vmem = pl.BlockSpec(memory_space=pltpu.VMEM)
    hbm = pl.BlockSpec(memory_space=pltpu.HBM)
    return pl.pallas_call(
        kernel,
        out_shape=out,
        in_specs=[SMEM] * len(scalars) + [vmem] * len(arrays) + [hbm] * len(far),
        out_specs=[hbm] * far_outs + [vmem] * (len(out) - far_outs) if isinstance(out, tuple) else vmem,
        scratch_shapes=scratch,
        compiler_params=pltpu.CompilerParams(vmem_limit_bytes=vmem_mib * 1024 * 1024),
        cost_estimate=pl.CostEstimate(flops=flops, bytes_accessed=moved, transcendentals=0),
        name=name,
    )(*scalars, *arrays, *far)


def exchange(strips):
    n = lax.axis_size("tiles")
    got = {0: strips[0]}
    for off, strip in zip(OFFSETS[1:], strips[1:]):
        got[-off] = lax.ppermute(strip, "tiles", [(i, (i + off) % n) for i in range(n)])
    return tuple(got[off] for off in OFFSETS)


def sum_of(pieces):
    return jnp.sum(pieces.astype(F32), axis=0)


def copies_of(piece, count):
    return jnp.broadcast_to(piece[None], (count, *piece.shape))


def group_exchange(pieces, groups):
    return lax.all_to_all(pieces, "tiles", 0, 0, tiled=True, axis_index_groups=groups)


def body(fields, neighbours, kernel, gain, w_in, w_out, cotangent):
    n_tiles, n_dp = lax.axis_size("tiles"), lax.axis_size("dp")
    slots = 2 * n_tiles
    own = (lax.axis_index("tiles").reshape(1).astype(jnp.int32),)
    tiles, cot = fields[0], cotangent[0]
    stage = pltpu.VMEM((2, SIZE * 16, 128), F32)
    sent = call(
        functools.partial(rim_kernel, slots=slots),
        "rims",
        STRIPS,
        own,
        (),
        (IDS, TILES, RIMS, stage, pltpu.SemaphoreType.DMA((3,)), STRIP_SEMS),
        far=(neighbours, tiles),
        far_outs=5,
        vmem_mib=60,
    )
    got = exchange(sent)
    share, grad, *sent = call(
        functools.partial(main_kernel, slots=slots),
        "main",
        (SHARE, jax.ShapeDtypeStruct((CELLS, CH), BF16), *STRIPS),
        own,
        (),
        MAIN_SCRATCH,
        far=(neighbours, *got, tiles, kernel, gain.reshape(1, CH), w_in, w_out, cot.reshape(CELLS, CH)),
        far_outs=7,
        flops=40 * 10**9,
        vmem_mib=60,
    )
    share = lax.all_to_all(share, "dp", 0, 0, tiled=True)
    share, got = lax.optimization_barrier((share, exchange(sent)))
    grad_fields = call(
        functools.partial(back_kernel, slots=slots),
        "back",
        jax.ShapeDtypeStruct((2, SIZE, SIZE, CH), BF16),
        own,
        (),
        (*LANDED, TILES, GRID_SPACE, NEAR, SPREAD, CONV, pltpu.SemaphoreType.DMA((9,))),
        far=(neighbours, *got, grad.reshape(tiles.shape), kernel, cot),
        flops=12 * 10**9,
        vmem_mib=60,
    )
    cut = call(sum_kernel, "sum_dp", jax.ShapeDtypeStruct(SHARE.shape[1:], BF16), (), (share,), vmem_mib=16)
    near = [list(range(g, g + NEAR_GROUP)) for g in range(0, n_tiles, NEAR_GROUP)]
    far = [list(range(g, n_tiles, NEAR_GROUP)) for g in range(NEAR_GROUP)]
    cut = group_exchange(cut.reshape(NEAR_GROUP, PIECE, 128), near)
    cut = group_exchange(copies_of(sum_of(cut), len(far[0])), far)
    cut, grad_fields = lax.optimization_barrier((cut, grad_fields))
    cut = group_exchange(copies_of(sum_of(cut).astype(BF16), NEAR_GROUP), near)
    scale = float((n_dp * slots * SIZE * SIZE) ** -0.5)
    g_in, g_out, g_taps, g_gain = call(
        functools.partial(last_kernel, scale=scale),
        "last",
        (
            jax.ShapeDtypeStruct((64, CH), F32),
            jax.ShapeDtypeStruct((64, CH), F32),
            jax.ShapeDtypeStruct((KW, KW, CH), F32),
            jax.ShapeDtypeStruct((1, CH), F32),
        ),
        (),
        (cut,),
        (pltpu.VMEM((2 * PART_ROWS, 128), F32),),
    )
    return grad_fields[None], g_in.T, g_out, g_taps, g_gain.reshape(CH)


def solution(mesh):
    return jax.shard_map(
        body,
        mesh=mesh,
        in_specs=(
            P("dp", "tiles", None, None, None),
            P("tiles", None),
            P(),
            P(),
            P(),
            P(),
            P("dp", "tiles", None, None, None),
        ),
        out_specs=(P("dp", "tiles", None, None, None), P(None, "dp"), P("dp", None), P(), P()),
        check_vma=False,
    )
```
